256 devices in a mesh: band: 8 (over x, y_hi), fft: 32 (over y_lo, z, core).
Axes of the slice: x: 4, y: 4 (y_hi: 2, y_lo: 2; y = y_hi * 2 + y_lo), z: 8, core: 2. Of those that a mesh axis runs over, the one named last changes fastest.
Arguments:
- orbitals: float32 [16, 128, 128, 128], P('band', 'fft'), may hold values from -6 to 6
- owners: int32 [4], replicated, may hold values from 0 to 15, as said below
- kernel: float32 [128, 128, 128], P(None, 'fft'), may hold values from 0.005 to 1, as said below
Outputs:
- exchange: float32 [16, 128, 128, 128], P('band', 'fft')
- projector: float32 [4, 128, 128, 128], P(None, 'fft', 'band')
The draws below stay inside these ranges and needn't reach their ends.
Inputs may be any that keep to these rules, and one draw needn't show every extreme that they name: `owners`: 4 distinct band indices, 0 and 15 among them. `kernel`: even: the value at indices (a, b, c) equals that at ((-a) mod 128, (-b) mod 128, (-c) mod 128).
All inputs are finite; a program needn't handle non-finite values.
Results may differ from the reference program's by a relative error of at most 0.0001.
Values sent between devices are 32-bit elements; how exact they have to be, the bound alone decides.
A program may use at most 64 MiB of HBM per device.

```python
import jax
import jax.numpy as jnp
from jax import lax

GRID = 128
ORB = 4
BANDS = 16


def draw_owners(key, part):
    key = jax.random.fold_in(key, 7)
    pick_key = jax.random.fold_in(key, 1)
    order_key = jax.random.fold_in(key, 2)
    ends = jnp.array([0, BANDS - 1], dtype=jnp.int32)
    if ORB > 2:
        inner = BANDS - 2
        scores = jax.random.randint(pick_key, (inner,), 0, 1 << 20, dtype=jnp.int32)
        distinct = scores * inner + jnp.arange(inner, dtype=jnp.int32)
        picked = lax.top_k(distinct, ORB - 2)[0]
        middle = (picked % inner + 1).astype(jnp.int32)
        chosen = jnp.concatenate([ends, middle])
    else:
        chosen = ends
    return jax.random.permutation(order_key, chosen).astype(jnp.int32)


def draw_kernel(key, part):
    key = jax.random.fold_in(key, 5)
    lowest = 0.02
    uniform_draw = jax.random.uniform(key, (GRID, GRID, GRID), jnp.float32)
    samples = jnp.exp(jnp.log(lowest) + uniform_draw * (0.0 - jnp.log(lowest)))
    mirror = jnp.roll(jnp.flip(samples, (0, 1, 2)), 1, (0, 1, 2))
    return (0.5 * (samples + mirror)).astype(jnp.float32)


def steps_of(key, dims, cuts, low, high):
    gain = 1.0
    for dim, blocks in cuts:
        heights = jax.random.uniform(jax.random.fold_in(jax.random.fold_in(key, 6), dim), (blocks,), jnp.float32, low / len(cuts), high / len(cuts))
        gain = gain * jnp.repeat(jnp.exp(heights), dims[dim] // blocks).reshape((-1,) + (1,) * (len(dims) - 1 - dim))
    return gain


def bell_draw(rng, shape, width, most, split=(), kind=jnp.bfloat16):
    entries = width * jax.random.normal(rng, shape, jnp.float32)
    if split:
        entries = entries * steps_of(rng, shape, split, -0.22, 0.18)
    return jnp.clip(entries, -most, most).astype(kind)


def setup_inputs(seed: int = 0) -> dict:
    key_of = jax.random.split(jax.random.key(seed), 4)
    return {
        "orbitals": bell_draw(key_of[0], (BANDS, GRID, GRID, GRID), 1.0, 6.0, ((0, 8), (1, 32)), jnp.float32),
        "owners": draw_owners(jax.random.fold_in(key_of[3], 71), 0),
        "kernel": draw_kernel(jax.random.fold_in(key_of[3], 71), 0),
    }


def potential_of(density, kernel):
    return jnp.real(jnp.fft.ifftn(kernel * jnp.fft.fftn(density))).astype(jnp.float32)


def reference(orbitals, owners, kernel):
    fetched = orbitals[owners.astype(jnp.int32)]

    def advance(accum, resident_band):
        fields = [potential_of(fetched[position] * resident_band, kernel) for position in range(ORB)]
        applied = jnp.zeros_like(resident_band)
        for position in range(ORB):
            applied = applied - fields[position] * fetched[position]
        accum = accum - jnp.stack(fields) * resident_band[None]
        return accum, applied

    start = jnp.zeros((ORB, GRID, GRID, GRID), jnp.float32)
    projector, exchange = lax.scan(advance, start, orbitals)
    return exchange, projector
```

```python
import functools

import jax
import jax.numpy as jnp
import ml_dtypes
import numpy as np
from jax import lax
from jax.experimental import pallas as pl
from jax.experimental.pallas import tpu as pltpu
from jax.sharding import PartitionSpec as P

MESH = pl.DeviceIdType.MESH
LEN = 128
COUNT = 4
GROUP = 32
BANDS = 8
PLANES = 4
ROWS = PLANES * LEN


def halves(table):
    high = table.astype(ml_dtypes.bfloat16)
    low = (table - high.astype(np.float64)).astype(ml_dtypes.bfloat16)
    return high, low


def tables():
    n = np.arange(LEN)
    angle = 2.0 * np.pi * ((n[:, None] * n[None, :]) % LEN) / LEN
    cos, sin = np.cos(angle), np.sin(angle)
    forward = np.block([[cos, sin], [-sin, cos]])
    inverse = np.block([[cos, -sin], [sin, cos]])
    natural = np.arange(2 * LEN).reshape(2, GROUP, PLANES)
    rows_y = natural.transpose(1, 0, 2).reshape(-1)
    rows_x = natural.transpose(1, 2, 0).reshape(-1)

    def left(table):
        high, low = halves(table)
        return np.concatenate([high, low, high], axis=1)

    def right(table):
        high, low = halves(table)
        return np.concatenate([high, low, high], axis=0)

    return (
        right(forward.T),
        left(forward[rows_y]),
        left(forward[:, rows_x]),
        left(inverse[rows_x]),
        left(inverse[:, rows_y]),
        right(inverse.T),
    )


def parts(values):
    high = values.astype(jnp.bfloat16)
    low = (values - high.astype(jnp.float32)).astype(jnp.bfloat16)
    return high, low


def apply_left(table, values):
    high, low = parts(values)
    return jnp.dot(table, jnp.concatenate([high, high, low], axis=0), preferred_element_type=jnp.float32)


def apply_right(values, table):
    high, low = parts(values)
    return jnp.dot(jnp.concatenate([high, high, low], axis=1), table, preferred_element_type=jnp.float32)


def kernel(
    owners, orb, kern, fwd_z, fwd_y, fwd_x, inv_x, inv_y, inv_z,
    exch, proj,
    masked, shares, fetched, c_send, c_recv, d_send, d_recv, partial, f_recv,
    s_send, s_recv, g_send, g_recv, cs_sem, cr_sem, ds_sem, dr_sem, fs_sem, fr_sem,
):
    band = lax.axis_index("band")
    pos = lax.axis_index("fft")
    slab = ROWS // BANDS
    block = PLANES * 8
    yrows = LEN // BANDS

    barrier = pltpu.get_barrier_semaphore()

    @pl.loop(1, BANDS)
    def _(k):
        pl.semaphore_signal(barrier, inc=1, device_id={"band": lax.rem(band + k, BANDS)}, device_id_type=MESH)

    @pl.loop(1, GROUP)
    def _(k):
        pl.semaphore_signal(barrier, inc=1, device_id={"fft": lax.rem(pos + k, GROUP)}, device_id_type=MESH)

    for i in range(COUNT):
        first = jnp.where(owners[i] == 2 * band, 1.0, 0.0)
        second = jnp.where(owners[i] == 2 * band + 1, 1.0, 0.0)
        masked[i] = first * orb[0] + second * orb[1]

    exch[...] = jnp.zeros_like(exch)
    pl.semaphore_wait(barrier, BANDS + GROUP - 2)

    def band_copy(src, dst, send, recv, target):
        return pltpu.make_async_remote_copy(
            src_ref=src, dst_ref=dst, send_sem=send, recv_sem=recv, device_id={"band": target}, device_id_type=MESH
        )

    def fft_copy(src, dst, send, recv, target):
        return pltpu.make_async_remote_copy(
            src_ref=src, dst_ref=dst, send_sem=send, recv_sem=recv, device_id={"fft": target}, device_id_type=MESH
        )

    def wait(ref, sem):
        pltpu.make_async_copy(ref, ref, sem).wait()

    mine = pl.ds(pl.multiple_of(band * slab, slab), slab)

    @pl.loop(0, COUNT)
    def _(i):
        @pl.loop(1, BANDS)
        def _(k):
            target = lax.rem(band + k, BANDS)
            theirs = pl.ds(pl.multiple_of(target * slab, slab), slab)
            band_copy(masked.at[i, theirs], shares.at[i, mine], s_send.at[i], s_recv.at[i], target).start()

        shares[i, mine] = masked[i, mine]

    @pl.loop(0, COUNT)
    def _(i):
        wait(shares.at[i, pl.ds(0, slab * (BANDS - 1))], s_recv.at[i])
        total = shares[i, pl.ds(0, slab)]
        for other in range(1, BANDS):
            total += shares[i, pl.ds(other * slab, slab)]
        fetched[i, mine] = total

        @pl.loop(1, BANDS)
        def _(k):
            target = lax.rem(band + k, BANDS)
            band_copy(fetched.at[i, mine], fetched.at[i, mine], g_send.at[i], g_recv.at[i], target).start()

    own = pl.ds(pl.multiple_of(pos * block, block), block)

    def exchange_blocks(send, recv, i, send_sem, recv_sem):
        @pl.loop(1, GROUP)
        def _(k):
            half = (k + 1) // 2
            step = jnp.where(k % 2 == 1, half, GROUP - half)
            target = lax.rem(pos + step, GROUP)
            theirs = pl.ds(pl.multiple_of(target * block, block), block)
            fft_copy(send.at[i, theirs], recv.at[i, own], send_sem.at[i], recv_sem.at[i], target).start()

        recv[i, own] = send[i, own]

    @pl.loop(0, COUNT + 2)
    def _(step):
        @pl.when(step < COUNT)
        def _():
            i = step
            wait(fetched.at[i, pl.ds(0, slab * (BANDS - 1))], g_recv.at[i])
            shared = fetched[i]
            density = jnp.concatenate([shared * orb[0], shared * orb[1]], axis=1)
            lines = apply_right(density, fwd_z[...])
            lines = lines.reshape(PLANES, LEN, 2 * LEN)
            stacked = jnp.concatenate(
                [jnp.concatenate([lines[p, :, :LEN], lines[p, :, LEN:]], axis=0) for p in range(PLANES)], axis=1
            )
            field = apply_left(fwd_y[...], stacked)
            out = jnp.stack([field[:, p * LEN : (p + 1) * LEN].reshape(GROUP, 8, LEN) for p in range(PLANES)], axis=1)
            c_send[i] = out.reshape(GROUP * block, LEN)
            exchange_blocks(c_send, c_recv, i, cs_sem, cr_sem)

        @pl.when((step >= 1) & (step < COUNT + 1))
        def _():
            i = step - 1
            wait(c_recv.at[i, pl.ds(0, block * (GROUP - 1))], cr_sem.at[i])
            columns = jnp.concatenate([c_recv[i, pl.ds(r, 2 * LEN, stride=4), :] for r in range(4)], axis=1)
            modes = apply_left(fwd_x[...], columns)
            scale = jnp.concatenate([kern[pl.ds(r, LEN, stride=4), :] for r in range(4)], axis=1) * (1.0 / LEN**3)
            modes = jnp.concatenate([modes[:LEN] * scale, modes[LEN:] * scale], axis=0)
            back = apply_left(inv_x[...], modes)
            for r in range(4):
                d_send[i, pl.ds(r, 2 * LEN, stride=4), :] = back[:, r * LEN : (r + 1) * LEN]
            exchange_blocks(d_send, d_recv, i, ds_sem, dr_sem)

        @pl.when(step >= 2)
        def _():
            i = step - 2
            wait(d_recv.at[i, pl.ds(0, block * (GROUP - 1))], dr_sem.at[i])
            rows = d_recv[i].reshape(GROUP, PLANES, 8, LEN)
            stacked = jnp.concatenate([rows[:, p].reshape(2 * LEN, LEN) for p in range(PLANES)], axis=1)
            lines = apply_left(inv_y[...], stacked)
            flat = jnp.concatenate(
                [
                    jnp.concatenate(
                        [lines[:LEN, p * LEN : (p + 1) * LEN], lines[LEN:, p * LEN : (p + 1) * LEN]], axis=1
                    )
                    for p in range(PLANES)
                ],
                axis=0,
            )
            field = apply_right(flat, inv_z[...])
            one, two = field[:, :LEN], field[:, LEN:]
            shared = fetched[i]
            exch[0] -= one * shared
            exch[1] -= two * shared
            partial[i] = (-(one * orb[0] + two * orb[1])).reshape(PLANES, LEN, LEN)

            @pl.loop(1, BANDS)
            def _(k):
                target = lax.rem(band + k, BANDS)
                theirs = pl.ds(pl.multiple_of(target * yrows, yrows), yrows)
                band_copy(partial.at[i, :, theirs], f_recv.at[i, band], fs_sem.at[i], fr_sem.at[i], target).start()

            f_recv[i, band] = partial[i, :, pl.ds(pl.multiple_of(band * yrows, yrows), yrows)]

    @pl.loop(0, COUNT)
    def _(i):
        wait(f_recv.at[i, pl.ds(0, BANDS - 1)], fr_sem.at[i])
        total = f_recv[i, 0]
        for other in range(1, BANDS):
            total += f_recv[i, other]
        proj[i] = total

    @pl.loop(0, COUNT)
    def _(i):
        wait(shares.at[i, pl.ds(0, slab * (BANDS - 1))], s_send.at[i])
        wait(fetched.at[i, pl.ds(0, slab * (BANDS - 1))], g_send.at[i])
        wait(c_send.at[i, pl.ds(0, block * (GROUP - 1))], cs_sem.at[i])
        wait(d_send.at[i, pl.ds(0, block * (GROUP - 1))], ds_sem.at[i])
        wait(f_recv.at[i, pl.ds(0, BANDS - 1)], fs_sem.at[i])


def shards(orbitals, owners, weights):
    vmem = pl.BlockSpec(memory_space=pltpu.VMEM)
    smem = pl.BlockSpec(memory_space=pltpu.SMEM)
    wide = pltpu.VMEM((COUNT, GROUP * PLANES * 8, LEN), jnp.float32)
    local = pltpu.VMEM((COUNT, ROWS, LEN), jnp.float32)
    sems = pltpu.SemaphoreType.DMA((COUNT,))
    exchange, projector = pl.pallas_call(
        kernel,
        out_shape=(
            jax.ShapeDtypeStruct((2, ROWS, LEN), jnp.float32),
            jax.ShapeDtypeStruct((COUNT, PLANES, LEN // BANDS, LEN), jnp.float32),
        ),
        in_specs=[smem] + [vmem] * 8,
        out_specs=(vmem, vmem),
        scratch_shapes=[
            local, local, local, wide, wide, wide, wide,
            pltpu.VMEM((COUNT, PLANES, LEN, LEN), jnp.float32),
            pltpu.VMEM((COUNT, BANDS, PLANES, LEN // BANDS, LEN), jnp.float32),
        ]
        + [sems] * 10,
        compiler_params=pltpu.CompilerParams(
            collective_id=0, has_side_effects=True, vmem_limit_bytes=48 * 2**20
        ),
        name="exchange",
    )(
        owners,
        orbitals.reshape(2, ROWS, LEN),
        weights.reshape(LEN * PLANES, LEN),
        *[jnp.asarray(table) for table in tables()],
    )
    return exchange.reshape(2, PLANES, LEN, LEN), projector


def solution(mesh):
    return jax.shard_map(
        shards,
        mesh=mesh,
        in_specs=(P("band", "fft", None, None), P(), P(None, "fft", None)),
        out_specs=(P("band", "fft", None, None), P(None, "fft", "band", None)),
        check_vma=False,
    )
```

```python
import functools

import jax
import jax.numpy as jnp
import ml_dtypes
import numpy as np
from jax import lax
from jax.experimental import pallas as pl
from jax.experimental.pallas import tpu as pltpu
from jax.sharding import PartitionSpec as P

MESH = pl.DeviceIdType.MESH
LEN = 128
COUNT = 4
GROUP = 32
BANDS = 8
PLANES = 4
ROWS = PLANES * LEN


def halves(table):
    high = table.astype(ml_dtypes.bfloat16)
    low = (table - high.astype(np.float64)).astype(ml_dtypes.bfloat16)
    return high, low


def tables():
    n = np.arange(LEN)
    angle = 2.0 * np.pi * ((n[:, None] * n[None, :]) % LEN) / LEN
    cos, sin = np.cos(angle), np.sin(angle)
    forward = np.block([[cos, sin], [-sin, cos]])
    inverse = np.block([[cos, -sin], [sin, cos]])
    natural = np.arange(2 * LEN).reshape(2, GROUP, PLANES)
    rows_y = natural.transpose(1, 0, 2).reshape(-1)
    rows_x = natural.transpose(1, 2, 0).reshape(-1)

    def left(table):
        high, low = halves(table)
        return np.concatenate([high, low, high], axis=1)

    def right(table):
        high, low = halves(table)
        return np.concatenate([high, low, high], axis=0)

    return (
        right(forward.T),
        left(forward[rows_y]),
        left(forward[:, rows_x]),
        left(inverse[rows_x]),
        left(inverse[:, rows_y]),
        right(inverse.T),
    )


def parts(values):
    high = values.astype(jnp.bfloat16)
    low = (values - high.astype(jnp.float32)).astype(jnp.bfloat16)
    return high, low


def apply_left(table, values):
    high, low = parts(values)
    return jnp.dot(table, jnp.concatenate([high, high, low], axis=0), preferred_element_type=jnp.float32)


def apply_right(values, table):
    high, low = parts(values)
    return jnp.dot(jnp.concatenate([high, high, low], axis=1), table, preferred_element_type=jnp.float32)


def kernel(
    owners_in, orb_in, kern_in, fwd_z_in, fwd_y_in, fwd_x_in, inv_x_in, inv_y_in, inv_z_in,
    exch, proj,
    owners, orb, kern, fwd_z, fwd_y, fwd_x, inv_x, inv_y, inv_z, load_sem,
    masked, shares, fetched, c_send, c_recv, d_send, d_recv, partial, f_recv,
    s_send, s_recv, g_send, g_recv, cs_sem, cr_sem, ds_sem, dr_sem, fs_sem, fr_sem,
):
    band = lax.axis_index("band")
    pos = lax.axis_index("fft")
    slab = ROWS // BANDS
    block = PLANES * 8
    yrows = LEN // BANDS

    loads = [
        pltpu.make_async_copy(src, dst, load_sem.at[k])
        for k, (src, dst) in enumerate(
            [(owners_in, owners), (orb_in, orb), (fwd_z_in, fwd_z), (fwd_y_in, fwd_y), (fwd_x_in, fwd_x), (kern_in, kern),
             (inv_x_in, inv_x), (inv_y_in, inv_y), (inv_z_in, inv_z)]
        )
    ]
    for load in loads:
        load.start()
    barrier = pltpu.get_barrier_semaphore()

    @pl.loop(1, BANDS)
    def _(k):
        pl.semaphore_signal(barrier, inc=1, device_id={"band": lax.rem(band + k, BANDS)}, device_id_type=MESH)

    @pl.loop(1, GROUP)
    def _(k):
        pl.semaphore_signal(barrier, inc=1, device_id={"fft": lax.rem(pos + k, GROUP)}, device_id_type=MESH)

    loads[0].wait()
    loads[1].wait()
    for i in range(COUNT):
        first = jnp.where(owners[i] == 2 * band, 1.0, 0.0)
        second = jnp.where(owners[i] == 2 * band + 1, 1.0, 0.0)
        masked[i] = first * orb[0] + second * orb[1]

    exch[...] = jnp.zeros_like(exch)
    pl.semaphore_wait(barrier, BANDS + GROUP - 2)

    def band_copy(src, dst, send, recv, target):
        return pltpu.make_async_remote_copy(
            src_ref=src, dst_ref=dst, send_sem=send, recv_sem=recv, device_id={"band": target}, device_id_type=MESH
        )

    def fft_copy(src, dst, send, recv, target):
        return pltpu.make_async_remote_copy(
            src_ref=src, dst_ref=dst, send_sem=send, recv_sem=recv, device_id={"fft": target}, device_id_type=MESH
        )

    def wait(ref, sem):
        pltpu.make_async_copy(ref, ref, sem).wait()

    mine = pl.ds(pl.multiple_of(band * slab, slab), slab)

    def scatter(i):
        @pl.loop(1, BANDS)
        def _(k):
            target = lax.rem(band + k, BANDS)
            theirs = pl.ds(pl.multiple_of(target * slab, slab), slab)
            band_copy(masked.at[i, theirs], shares.at[i, mine], s_send.at[i], s_recv.at[i], target).start()

        shares[i, mine] = masked[i, mine]

    def gather(i):
        wait(shares.at[i, pl.ds(0, slab * (BANDS - 1))], s_recv.at[i])
        total = shares[i, pl.ds(0, slab)]
        for other in range(1, BANDS):
            total += shares[i, pl.ds(other * slab, slab)]
        fetched[i, mine] = total

        @pl.loop(1, BANDS)
        def _(k):
            target = lax.rem(band + k, BANDS)
            band_copy(fetched.at[i, mine], fetched.at[i, mine], g_send.at[i], g_recv.at[i], target).start()

    scatter(0)
    gather(0)
    scatter(1)
    for load in loads[2:]:
        load.wait()

    own = pl.ds(pl.multiple_of(pos * block, block), block)

    def exchange_blocks(send, recv, i, send_sem, recv_sem):
        @pl.loop(1, GROUP)
        def _(k):
            half = (k + 1) // 2
            step = jnp.where(k % 2 == 1, half, GROUP - half)
            target = lax.rem(pos + step, GROUP)
            theirs = pl.ds(pl.multiple_of(target * block, block), block)
            fft_copy(send.at[i, theirs], recv.at[i, own], send_sem.at[i], recv_sem.at[i], target).start()

        recv[i, own] = send[i, own]

    @pl.loop(0, COUNT + 2)
    def _(step):
        @pl.when(step < COUNT)
        def _():
            i = step
            wait(fetched.at[i, pl.ds(0, slab * (BANDS - 1))], g_recv.at[i])
            shared = fetched[i]
            density = jnp.concatenate([shared * orb[0], shared * orb[1]], axis=1)
            lines = apply_right(density, fwd_z[...])
            lines = lines.reshape(PLANES, LEN, 2 * LEN)
            stacked = jnp.concatenate(
                [jnp.concatenate([lines[p, :, :LEN], lines[p, :, LEN:]], axis=0) for p in range(PLANES)], axis=1
            )
            field = apply_left(fwd_y[...], stacked)
            out = jnp.stack([field[:, p * LEN : (p + 1) * LEN].reshape(GROUP, 8, LEN) for p in range(PLANES)], axis=1)
            c_send[i] = out.reshape(GROUP * block, LEN)
            exchange_blocks(c_send, c_recv, i, cs_sem, cr_sem)

            @pl.when(step < COUNT - 1)
            def _():
                gather(step + 1)

            @pl.when(step < COUNT - 2)
            def _():
                scatter(step + 2)

        @pl.when((step >= 1) & (step < COUNT + 1))
        def _():
            i = step - 1
            wait(c_recv.at[i, pl.ds(0, block * (GROUP - 1))], cr_sem.at[i])
            columns = jnp.concatenate([c_recv[i, pl.ds(r, 2 * LEN, stride=4), :] for r in range(4)], axis=1)
            modes = apply_left(fwd_x[...], columns)
            scale = jnp.concatenate([kern[pl.ds(r, LEN, stride=4), :] for r in range(4)], axis=1) * (1.0 / LEN**3)
            modes = jnp.concatenate([modes[:LEN] * scale, modes[LEN:] * scale], axis=0)
            back = apply_left(inv_x[...], modes)
            for r in range(4):
                d_send[i, pl.ds(r, 2 * LEN, stride=4), :] = back[:, r * LEN : (r + 1) * LEN]
            exchange_blocks(d_send, d_recv, i, ds_sem, dr_sem)

        @pl.when(step >= 2)
        def _():
            i = step - 2
            wait(d_recv.at[i, pl.ds(0, block * (GROUP - 1))], dr_sem.at[i])
            rows = d_recv[i].reshape(GROUP, PLANES, 8, LEN)
            stacked = jnp.concatenate([rows[:, p].reshape(2 * LEN, LEN) for p in range(PLANES)], axis=1)
            lines = apply_left(inv_y[...], stacked)
            flat = jnp.concatenate(
                [
                    jnp.concatenate(
                        [lines[:LEN, p * LEN : (p + 1) * LEN], lines[LEN:, p * LEN : (p + 1) * LEN]], axis=1
                    )
                    for p in range(PLANES)
                ],
                axis=0,
            )
            field = apply_right(flat, inv_z[...])
            one, two = field[:, :LEN], field[:, LEN:]
            shared = fetched[i]
            exch[0] -= one * shared
            exch[1] -= two * shared
            partial[i] = (-(one * orb[0] + two * orb[1])).reshape(PLANES, LEN, LEN)

            @pl.loop(1, BANDS)
            def _(k):
                target = lax.rem(band + k, BANDS)
                theirs = pl.ds(pl.multiple_of(target * yrows, yrows), yrows)
                band_copy(partial.at[i, :, theirs], f_recv.at[i, band], fs_sem.at[i], fr_sem.at[i], target).start()

            f_recv[i, band] = partial[i, :, pl.ds(pl.multiple_of(band * yrows, yrows), yrows)]

    @pl.loop(0, COUNT)
    def _(i):
        wait(f_recv.at[i, pl.ds(0, BANDS - 1)], fr_sem.at[i])
        total = f_recv[i, 0]
        for other in range(1, BANDS):
            total += f_recv[i, other]
        proj[i] = total

    @pl.loop(0, COUNT)
    def _(i):
        wait(shares.at[i, pl.ds(0, slab * (BANDS - 1))], s_send.at[i])
        wait(fetched.at[i, pl.ds(0, slab * (BANDS - 1))], g_send.at[i])
        wait(c_send.at[i, pl.ds(0, block * (GROUP - 1))], cs_sem.at[i])
        wait(d_send.at[i, pl.ds(0, block * (GROUP - 1))], ds_sem.at[i])
        wait(f_recv.at[i, pl.ds(0, BANDS - 1)], fs_sem.at[i])


def shards(orbitals, owners, weights):
    vmem = pl.BlockSpec(memory_space=pltpu.VMEM)
    wide = pltpu.VMEM((COUNT, GROUP * PLANES * 8, LEN), jnp.float32)
    local = pltpu.VMEM((COUNT, ROWS, LEN), jnp.float32)
    tall = pltpu.VMEM((6 * LEN, 2 * LEN), jnp.bfloat16)
    flat = pltpu.VMEM((2 * LEN, 6 * LEN), jnp.bfloat16)
    sems = pltpu.SemaphoreType.DMA((COUNT,))
    exchange, projector = pl.pallas_call(
        kernel,
        out_shape=(
            jax.ShapeDtypeStruct((2, ROWS, LEN), jnp.float32),
            jax.ShapeDtypeStruct((COUNT, PLANES, LEN // BANDS, LEN), jnp.float32),
        ),
        in_specs=[pl.BlockSpec(memory_space=pltpu.HBM)] * 9,
        out_specs=(vmem, vmem),
        scratch_shapes=[
            pltpu.SMEM((COUNT,), jnp.int32),
            pltpu.VMEM((2, ROWS, LEN), jnp.float32),
            pltpu.VMEM((ROWS, LEN), jnp.float32),
            tall, flat, flat, flat, flat, tall,
            pltpu.SemaphoreType.DMA((9,)),
            local, local, local, wide, wide, wide, wide,
            pltpu.VMEM((COUNT, PLANES, LEN, LEN), jnp.float32),
            pltpu.VMEM((COUNT, BANDS, PLANES, LEN // BANDS, LEN), jnp.float32),
        ]
        + [sems] * 10,
        compiler_params=pltpu.CompilerParams(
            collective_id=0, has_side_effects=True, vmem_limit_bytes=64 * 2**20 - 2**16
        ),
        name="exchange",
    )(
        owners,
        orbitals.reshape(2, ROWS, LEN),
        weights.reshape(LEN * PLANES, LEN),
        *[jnp.asarray(table) for table in tables()],
    )
    return exchange.reshape(2, PLANES, LEN, LEN), projector


def solution(mesh):
    return jax.shard_map(
        shards,
        mesh=mesh,
        in_specs=(P("band", "fft", None, None), P(), P(None, "fft", None)),
        out_specs=(P("band", "fft", None, None), P(None, "fft", "band", None)),
        check_vma=False,
    )
```

```python
import functools

import jax
import jax.numpy as jnp
import ml_dtypes
import numpy as np
from jax import lax
from jax.experimental import pallas as pl
from jax.experimental.pallas import tpu as pltpu
from jax.sharding import PartitionSpec as P

MESH = pl.DeviceIdType.MESH
LEN = 128
COUNT = 4
GROUP = 32
BANDS = 8
PLANES = 4
ROWS = PLANES * LEN


def halves(table):
    high = table.astype(ml_dtypes.bfloat16)
    low = (table - high.astype(np.float64)).astype(ml_dtypes.bfloat16)
    return high, low


def tables():
    n = np.arange(LEN)
    angle = 2.0 * np.pi * ((n[:, None] * n[None, :]) % LEN) / LEN
    cos, sin = np.cos(angle), np.sin(angle)
    forward = np.block([[cos, sin], [-sin, cos]])
    inverse = np.block([[cos, -sin], [sin, cos]])
    rows_y = np.arange(2 * LEN).reshape(2, GROUP, PLANES).transpose(1, 0, 2).reshape(-1)
    place, j = np.arange(GROUP)[:, None], np.arange(PLANES)[None, :]
    x, y_hi, y_lo, core = place // 8, place // 4 % 2, place // 2 % 2, place % 2
    plane = 64 * y_lo + 8 * (2 * j + 1 - core) + 4 * y_hi + x
    rows_x = np.stack([plane, plane + LEN], axis=-1).reshape(-1)

    def left(table):
        high, low = halves(table)
        return np.concatenate([high, low, high], axis=1)

    def right(table):
        high, low = halves(table)
        return np.concatenate([high, low, high], axis=0)

    return (
        right(forward.T),
        left(forward[rows_y]),
        left(forward[:, rows_x]),
        left(inverse[rows_x]),
        left(inverse[:, rows_y]),
        right(inverse.T),
    )


def parts(values):
    high = values.astype(jnp.bfloat16)
    low = (values - high.astype(jnp.float32)).astype(jnp.bfloat16)
    return high, low


def apply_left(table, values):
    high, low = parts(values)
    return jnp.dot(table, jnp.concatenate([high, high, low], axis=0), preferred_element_type=jnp.float32)


def apply_right(values, table):
    high, low = parts(values)
    return jnp.dot(jnp.concatenate([high, high, low], axis=1), table, preferred_element_type=jnp.float32)


def kernel(
    owners_in, orb_in, kern_in, fwd_z_in, fwd_y_in, fwd_x_in, inv_x_in, inv_y_in, inv_z_in,
    exch, proj,
    owners, orb, kern_own, fwd_z, fwd_y, fwd_x, inv_x, inv_y, inv_z, load_sem,
    res, inter, chosen, kern, fetched, c_send, c_recv, d_send, d_recv, total, back_recv, partial, f_recv, shared_sum, p_recv, br_sem,
    as_sem, ar_sem, bs_sem, ks_sem, kr_sem, es_sem, er_sem,
    gs_sem, gr_sem, cs_sem, cr_sem, ds_sem, dr_sem, fs_sem, fr_sem, ps_sem, pr_sem,
):
    band = lax.axis_index("band")
    pos = lax.axis_index("fft")
    x, y_hi = band // 2, band % 2
    y_lo, z, core = pos // 16, pos // 2 % 8, pos % 2
    half = LEN // 2
    block = PLANES * 8
    yrows = LEN // BANDS

    def device(to_band, to_y_lo, to_z, to_core):
        return (to_band, 16 * to_y_lo + 2 * to_z + to_core)

    def remote(src, dst, send, recv, target):
        return pltpu.make_async_remote_copy(
            src_ref=src, dst_ref=dst, send_sem=send, recv_sem=recv, device_id=target, device_id_type=MESH
        )

    def wait(ref, sem):
        pltpu.make_async_copy(ref, ref, sem).wait()

    def rows(index, size):
        return pl.ds(pl.multiple_of(index * size, size), size)

    loads = [
        pltpu.make_async_copy(src, dst, load_sem.at[k])
        for k, (src, dst) in enumerate(
            [(orb_in, orb), (owners_in, owners), (kern_in, kern_own), (fwd_z_in, fwd_z), (fwd_y_in, fwd_y),
             (fwd_x_in, fwd_x), (inv_x_in, inv_x), (inv_y_in, inv_y), (inv_z_in, inv_z)]
        )
    ]
    for load in loads:
        load.start()

    place = 4 * band + 2 * y_lo + core
    mine = 16 * y_lo + 2 * ((band - z + 8) % 8) + core

    barrier = pltpu.get_barrier_semaphore()

    def greet(target):
        pl.semaphore_signal(barrier, inc=1, device_id=target, device_id_type=MESH)

    @pl.loop(1, GROUP)
    def _(k):
        other = (place + k) % GROUP
        greet(device(other // 4, other // 2 % 2, z, other % 2))

    @pl.loop(1, 16)
    def _(k):
        other = (2 * z + core + k) % 16
        greet((band, 16 * y_lo + other))

    for load in loads[:3]:
        load.wait()
    total[...] = jnp.zeros_like(total)
    pl.semaphore_wait(barrier, GROUP - 1 + 15)

    mirror = (band - z + 8) % 8

    @pl.when(mirror == z)
    def _():
        pltpu.make_async_copy(kern_own, kern, kr_sem).start()

    @pl.when(mirror != z)
    def _():
        remote(kern_own, kern, ks_sem, kr_sem, device(band, y_lo, mirror, core)).start()

    for step in (2, 1, 3, 0):
        r = (x + step) % PLANES
        for h in range(2):
            src = orb.at[:, rows(2 * r + h, half)]
            dst = inter.at[rows(band, 2)]
            local = (band == 2 * r + core) & (core == h)

            @pl.when(local)
            def _():
                pltpu.make_async_copy(src, dst, br_sem.at[band]).start()

            @pl.when(jnp.logical_not(local))
            def _():
                remote(src, dst, bs_sem, br_sem.at[band], device(2 * r + core, y_lo, z, h)).start()

    def to_planes(odd, src, dst, send, recv):
        target_core = 1 - z % 2
        for step in range(4):
            to = 2 * ((z // 2 + 2 + step) % 4) + odd
            local = (to == z) & (target_core == core)

            @pl.when(local)
            def _():
                pltpu.make_async_copy(src(to), dst, recv).start()

            @pl.when(jnp.logical_not(local))
            def _():
                remote(src(to), dst, send, recv, device(band, y_lo, to, target_core)).start()

    slot = rows(2 * (z // 2) + core, half)

    def select(i):
        chosen[i] = inter[owners[i]]

    def spread(i, odd):
        to_planes(odd, lambda to: chosen.at[i], fetched.at[i, slot], gs_sem.at[i], gr_sem.at[i])

    def arrived(odd):
        for step in range(4):
            source = 2 * step + odd
            wait(inter.at[rows(source, 2)], br_sem.at[source])

    def resident(odd):
        to_planes(odd, lambda to: inter.at[rows(to, 2)], res.at[:, slot], as_sem, ar_sem)

    arrived(0)
    resident(0)
    arrived(1)
    select(0)
    spread(0, 0)
    resident(1)
    spread(0, 1)
    for load in loads[3:]:
        load.wait()

    select(1)
    spread(1, 0)
    spread(1, 1)
    wait(res, ar_sem)

    @pl.loop(0, COUNT + 3)
    def _(step):
        @pl.when(step < COUNT)
        def _():
            i = step
            wait(fetched.at[i], gr_sem.at[i])
            shared = fetched[i]
            density = jnp.concatenate([shared * res[0], shared * res[1]], axis=1)
            lines = apply_right(density, fwd_z[...])
            lines = lines.reshape(PLANES, LEN, 2 * LEN)
            stacked = jnp.concatenate(
                [jnp.concatenate([lines[p, :, :LEN], lines[p, :, LEN:]], axis=0) for p in range(PLANES)], axis=1
            )
            field = apply_left(fwd_y[...], stacked)
            out = jnp.stack([field[:, p * LEN : (p + 1) * LEN].reshape(GROUP, 8, LEN) for p in range(PLANES)], axis=1)
            c_send[i] = out.reshape(GROUP * block, LEN)

            @pl.loop(1, GROUP)
            def _(k):
                other = (mine + 11 * k) % GROUP
                remote(
                    c_send.at[i, rows(other, block)], c_recv.at[i, rows(place, block)], cs_sem.at[i], cr_sem.at[i],
                    device((other // 2 % 8 + z) % 8, other // 16, z, other % 2),
                ).start()

            c_recv[i, rows(place, block)] = c_send[i, rows(mine, block)]

            @pl.when(step < COUNT - 2)
            def _():
                select(step + 2)
                spread(step + 2, 0)
                spread(step + 2, 1)

        @pl.when((step >= 1) & (step < COUNT + 1))
        def _():
            i = step - 1

            @pl.when(i == 0)
            def _():
                wait(kern, kr_sem)

            wait(c_recv.at[i, pl.ds(0, block * (GROUP - 1))], cr_sem.at[i])
            columns = jnp.concatenate([c_recv[i, pl.ds(r, 2 * LEN, stride=4), :] for r in range(4)], axis=1)
            modes = apply_left(fwd_x[...], columns)
            scale = jnp.concatenate([kern[pl.ds(r, LEN, stride=4), :] for r in range(4)], axis=1) * (1.0 / LEN**3)
            modes = jnp.concatenate([modes[:LEN] * scale, modes[LEN:] * scale], axis=0)
            back = apply_left(inv_x[...], modes)
            for r in range(4):
                d_send[i, pl.ds(r, 2 * LEN, stride=4), :] = back[:, r * LEN : (r + 1) * LEN]

            @pl.loop(1, GROUP)
            def _(k):
                other = (place + 11 * k) % GROUP
                remote(
                    d_send.at[i, rows(other, block)], d_recv.at[i, rows(mine, block)], ds_sem.at[i], dr_sem.at[i],
                    device(other // 4, other // 2 % 2, z, other % 2),
                ).start()

            d_recv[i, rows(mine, block)] = d_send[i, rows(place, block)]

        @pl.when((step >= 2) & (step < COUNT + 2))
        def _():
            i = step - 2
            wait(d_recv.at[i, pl.ds(0, block * (GROUP - 1))], dr_sem.at[i])
            tiles = d_recv[i].reshape(GROUP, PLANES, 8, LEN)
            stacked = jnp.concatenate([tiles[:, p].reshape(2 * LEN, LEN) for p in range(PLANES)], axis=1)
            lines = apply_left(inv_y[...], stacked)
            flat = jnp.concatenate(
                [
                    jnp.concatenate(
                        [lines[:LEN, p * LEN : (p + 1) * LEN], lines[LEN:, p * LEN : (p + 1) * LEN]], axis=1
                    )
                    for p in range(PLANES)
                ],
                axis=0,
            )
            field = apply_right(flat, inv_z[...])
            one, two = field[:, :LEN], field[:, LEN:]
            shared = fetched[i]
            total[0] -= one * shared
            total[1] -= two * shared

            @pl.when(i == COUNT - 1)
            def _():
                for step_z in (2, 1, 3, 0):
                    j = (z // 2 + step_z) % PLANES
                    remote(
                        total.at[:, rows(j, LEN)], back_recv.at[:, rows(x, LEN)], es_sem, er_sem,
                        device(z, y_lo, 2 * j + 1 - core, y_hi),
                    ).start()

            partial[i] = -(one * res[0] + two * res[1])

            @pl.loop(0, 2 * PLANES)
            def _(k):
                j, to_core = (z // 2 + 2 + k // 2) % PLANES, k % 2
                to_z = 2 * j + 1 - core
                src = partial.at[i, rows(2 * j + to_core, half)]
                dst = f_recv.at[i, z]
                local = (to_z == z) & (to_core == core)

                @pl.when(local)
                def _():
                    pltpu.make_async_copy(src, dst, fr_sem.at[i]).start()

                @pl.when(jnp.logical_not(local))
                def _():
                    remote(src, dst, fs_sem.at[i], fr_sem.at[i], device(band, y_lo, to_z, to_core)).start()

        @pl.when(step >= 3)
        def _():
            i = step - 3
            wait(f_recv.at[i], fr_sem.at[i])
            summed = f_recv[i, 0]
            for other in range(1, 8):
                summed += f_recv[i, other]
            shared_sum[i] = summed

            @pl.loop(0, 4)
            def _(k):
                to = 4 * core + k
                src = shared_sum.at[i, rows(k, yrows)]
                dst = p_recv.at[i, x]
                local = (to == band) & (y_hi == core)

                @pl.when(local)
                def _():
                    pltpu.make_async_copy(src, dst, pr_sem.at[i]).start()

                @pl.when(jnp.logical_not(local))
                def _():
                    remote(src, dst, ps_sem.at[i], pr_sem.at[i], device(to, y_lo, z, y_hi)).start()

    @pl.loop(0, COUNT)
    def _(i):
        wait(p_recv.at[i], pr_sem.at[i])
        proj[i] = p_recv[i]

    wait(back_recv, er_sem)
    exch[...] = back_recv[...]

    wait(total, es_sem)

    @pl.when(core == y_hi)
    def _():
        wait(inter.at[pl.ds(0, 14)], bs_sem)

    @pl.when(core != y_hi)
    def _():
        wait(inter, bs_sem)

    @pl.when(mirror != z)
    def _():
        wait(kern, ks_sem)

    @pl.when(core == 1 - z % 2)
    def _():
        wait(inter.at[pl.ds(0, 14)], as_sem)

    @pl.when(core == z % 2)
    def _():
        wait(inter, as_sem)

    @pl.loop(0, COUNT)
    def _(i):
        @pl.when(core == 1 - z % 2)
        def _():
            wait(fetched.at[i, pl.ds(0, 7 * half)], gs_sem.at[i])

        @pl.when(core == z % 2)
        def _():
            wait(fetched.at[i], gs_sem.at[i])

        wait(c_send.at[i, pl.ds(0, block * (GROUP - 1))], cs_sem.at[i])
        wait(d_send.at[i, pl.ds(0, block * (GROUP - 1))], ds_sem.at[i])

        @pl.when(core == 1 - z % 2)
        def _():
            wait(partial.at[i, pl.ds(0, ROWS - half)], fs_sem.at[i])

        @pl.when(core == z % 2)
        def _():
            wait(partial.at[i], fs_sem.at[i])

        @pl.when((core == band // 4) & (core == y_hi))
        def _():
            wait(p_recv.at[i, pl.ds(0, 3)], ps_sem.at[i])

        @pl.when((core != band // 4) | (core != y_hi))
        def _():
            wait(p_recv.at[i], ps_sem.at[i])


def shards(orbitals, owners, weights):
    vmem = pl.BlockSpec(memory_space=pltpu.VMEM)
    wide = pltpu.VMEM((COUNT, GROUP * PLANES * 8, LEN), jnp.float32)
    local = pltpu.VMEM((COUNT, ROWS, LEN), jnp.float32)
    pair = pltpu.VMEM((2, ROWS, LEN), jnp.float32)
    single = pltpu.VMEM((ROWS, LEN), jnp.float32)
    tall = pltpu.VMEM((6 * LEN, 2 * LEN), jnp.bfloat16)
    flat = pltpu.VMEM((2 * LEN, 6 * LEN), jnp.bfloat16)
    sem = pltpu.SemaphoreType.DMA
    sems = pltpu.SemaphoreType.DMA((COUNT,))
    exchange, projector = pl.pallas_call(
        kernel,
        out_shape=(
            jax.ShapeDtypeStruct((2, ROWS, LEN), jnp.float32),
            jax.ShapeDtypeStruct((COUNT, PLANES, LEN // BANDS, LEN), jnp.float32),
        ),
        in_specs=[pl.BlockSpec(memory_space=pltpu.HBM)] * 9,
        out_specs=(vmem, vmem),
        scratch_shapes=[
            pltpu.SMEM((COUNT,), jnp.int32), pair, single,
            tall, flat, flat, flat, flat, tall,
            pltpu.SemaphoreType.DMA((9,)),
            pair,
            pltpu.VMEM((2 * BANDS, LEN // 2, LEN), jnp.float32),
            pltpu.VMEM((COUNT, LEN // 2, LEN), jnp.float32),
            single, local, wide, wide, wide, wide, pair, pair, local,
            pltpu.VMEM((COUNT, 8, LEN // 2, LEN), jnp.float32),
            pltpu.VMEM((COUNT, LEN // 2, LEN), jnp.float32),
            pltpu.VMEM((COUNT, PLANES, LEN // BANDS, LEN), jnp.float32),
            pltpu.SemaphoreType.DMA((8,)),
        ]
        + [sem] * 7
        + [sems] * 10,
        compiler_params=pltpu.CompilerParams(
            collective_id=0, has_side_effects=True, vmem_limit_bytes=64 * 2**20 - 2**16
        ),
        name="exchange",
    )(
        owners,
        orbitals.reshape(2, ROWS, LEN),
        weights.reshape(LEN * PLANES, LEN),
        *[jnp.asarray(table) for table in tables()],
    )
    return exchange.reshape(2, PLANES, LEN, LEN), projector


def solution(mesh):
    return jax.shard_map(
        shards,
        mesh=mesh,
        in_specs=(P("band", "fft", None, None), P(), P(None, "fft", None)),
        out_specs=(P("band", "fft", None, None), P(None, "fft", "band", None)),
        check_vma=False,
    )
```

```python
import functools

import jax
import jax.numpy as jnp
import ml_dtypes
import numpy as np
from jax import lax
from jax.experimental import pallas as pl
from jax.experimental.pallas import tpu as pltpu
from jax.sharding import PartitionSpec as P

MESH = pl.DeviceIdType.MESH
LEN = 128
COUNT = 4
GROUP = 32
BANDS = 8
ORDER = ((2, 2), (2, 1), (1, 2), (2, 3), (3, 2), (2, 0), (0, 2), (1, 1), (3, 3), (1, 3), (3, 1), (1, 0), (0, 1), (3, 0), (0, 3), (0, 0))
PLANES = 4
ROWS = PLANES * LEN


def halves(table):
    high = table.astype(ml_dtypes.bfloat16)
    low = (table - high.astype(np.float64)).astype(ml_dtypes.bfloat16)
    return high, low


def tables():
    n = np.arange(LEN)
    angle = 2.0 * np.pi * ((n[:, None] * n[None, :]) % LEN) / LEN
    cos, sin = np.cos(angle), np.sin(angle)
    forward = np.block([[cos, sin], [-sin, cos]])
    inverse = np.block([[cos, -sin], [sin, cos]])
    rows_y = np.arange(2 * LEN).reshape(2, GROUP, PLANES).transpose(1, 0, 2).reshape(-1)
    place, j = np.arange(GROUP)[:, None], np.arange(PLANES)[None, :]
    x, y_hi, y_lo, core = place // 8, place // 4 % 2, place // 2 % 2, place % 2
    plane = 64 * y_lo + 8 * (2 * j + 1 - core) + 4 * y_hi + x
    rows_x = np.stack([plane, plane + LEN], axis=-1).reshape(-1)

    def left(table):
        high, low = halves(table)
        return np.concatenate([high, low, high], axis=1)

    def right(table):
        high, low = halves(table)
        return np.concatenate([high, low, high], axis=0)

    return (
        right(forward.T),
        left(forward[rows_y]),
        left(forward[:, rows_x]),
        left(inverse[rows_x]),
        left(inverse[:, rows_y]),
        right(inverse.T),
    )


def parts(values):
    high = values.astype(jnp.bfloat16)
    low = (values - high.astype(jnp.float32)).astype(jnp.bfloat16)
    return high, low


def apply_left(table, values):
    high, low = parts(values)
    return jnp.dot(table, jnp.concatenate([high, high, low], axis=0), preferred_element_type=jnp.float32)


def apply_right(values, table):
    high, low = parts(values)
    return jnp.dot(jnp.concatenate([high, high, low], axis=1), table, preferred_element_type=jnp.float32)


def kernel(
    owners_in, orb_in, kern_in, fwd_z_in, fwd_y_in, fwd_x_in, inv_x_in, inv_y_in, inv_z_in,
    exch, proj,
    owners, orb, kern_own, fwd_z, fwd_y, fwd_x, inv_x, inv_y, inv_z, load_sem,
    res, inter, chosen, kern, fetched, c_send, c_recv, d_send, d_recv, total, back_recv, partial, f_recv, shared_sum, p_recv, br_sem,
    as_sem, ar_sem, bs_sem, ks_sem, kr_sem, es_sem, er_sem,
    gs_sem, gr_sem, cs_sem, cr_sem, ds_sem, dr_sem, fs_sem, fr_sem, ps_sem, pr_sem,
):
    band = lax.axis_index("band")
    pos = lax.axis_index("fft")
    x, y_hi = band // 2, band % 2
    y_lo, z, core = pos // 16, pos // 2 % 8, pos % 2
    half = LEN // 2
    turn = 1 - 2 * core
    block = PLANES * 8
    yrows = LEN // BANDS

    def device(to_band, to_y_lo, to_z, to_core):
        return (to_band, 16 * to_y_lo + 2 * to_z + to_core)

    def remote(src, dst, send, recv, target):
        return pltpu.make_async_remote_copy(
            src_ref=src, dst_ref=dst, send_sem=send, recv_sem=recv, device_id=target, device_id_type=MESH
        )

    def wait(ref, sem):
        pltpu.make_async_copy(ref, ref, sem).wait()

    def rows(index, size):
        return pl.ds(pl.multiple_of(index * size, size), size)

    loads = [
        pltpu.make_async_copy(src, dst, load_sem.at[k])
        for k, (src, dst) in enumerate(
            [(orb_in, orb), (owners_in, owners), (kern_in, kern_own), (fwd_z_in, fwd_z), (fwd_y_in, fwd_y),
             (fwd_x_in, fwd_x), (inv_x_in, inv_x), (inv_y_in, inv_y), (inv_z_in, inv_z)]
        )
    ]
    for load in loads:
        load.start()

    place = 4 * band + 2 * y_lo + core
    mine = 16 * y_lo + 2 * ((band - z + 8) % 8) + core

    barrier = pltpu.get_barrier_semaphore()

    def greet(target):
        pl.semaphore_signal(barrier, inc=1, device_id=target, device_id_type=MESH)

    def wrap(value, size):
        return jnp.where(value >= size, value - size, value)

    others = []
    step_by = jnp.where(core == 0, 1, 3)
    x_at = [x, wrap(x + step_by, 4), wrap(x + 2, 4), wrap(x + 4 - step_by, 4)]
    y_all = 2 * y_hi + y_lo
    y_at = []
    for value in (y_all, wrap(y_all + step_by, 4), wrap(y_all + 2, 4), wrap(y_all + 4 - step_by, 4)):
        upper = jnp.where(value >= 2, 1, 0)
        y_at.append((upper, value - 2 * upper))
    for dx, dy in ORDER:
        to_band = 2 * x_at[dx] + y_at[dy][0]
        to_y_lo = y_at[dy][1]
        to_zeta = wrap(to_band + 8 - z, 8)
        for flip in range(2):
            if (dx, dy, flip) != (0, 0, 0):
                to_core = core if flip == 0 else 1 - core
                others.append((
                    (to_band, 16 * to_y_lo + 2 * z + to_core),
                    4 * to_band + 2 * to_y_lo + to_core,
                    16 * to_y_lo + 2 * to_zeta + to_core,
                ))

    for target, _, _ in others:
        greet(target)

    @pl.loop(1, 16)
    def _(k):
        other = (2 * z + core + k) % 16
        greet((band, 16 * y_lo + other))

    greet(device((band + 4) % BANDS, y_lo, (band - z + 8) % 8, core))
    for load in loads[:3]:
        load.wait()
    total[...] = jnp.zeros_like(total)
    pl.semaphore_wait(barrier, GROUP - 1 + 15 + 1)

    mirror = (band - z + 8) % 8
    across = (band + 4) % BANDS
    near, far = pl.ds(0, ROWS // 2), pl.ds(ROWS // 2, ROWS // 2)
    remote(
        kern_own.at[far], kern.at[far], ks_sem.at[1], kr_sem.at[1], device(across, y_lo, (across - z + 8) % 8, core)
    ).start()

    @pl.when(mirror == z)
    def _():
        pltpu.make_async_copy(kern_own.at[near], kern.at[near], kr_sem.at[0]).start()

    @pl.when(mirror != z)
    def _():
        remote(
            kern_own.at[near], kern.at[near], ks_sem.at[0], kr_sem.at[0], device(band, y_lo, mirror, core)
        ).start()

    for a in range(2):
        for step in (2, 1, 3, 0):
            r = (x + turn * step + PLANES) % PLANES
            for h in range(2):
                src = orb.at[a, rows(2 * r + h, half)]
                dst = inter.at[2 * band + a]
                local = (band == 2 * r + core) & (core == h)

                @pl.when(local)
                def _():
                    pltpu.make_async_copy(src, dst, br_sem.at[a, band]).start()

                @pl.when(jnp.logical_not(local))
                def _():
                    remote(src, dst, bs_sem, br_sem.at[a, band], device(2 * r + core, y_lo, z, h)).start()

    def to_planes(odd, src, dst, send, recv):
        target_core = 1 - z % 2
        for step in range(4):
            to = 2 * ((z // 2 + 6 + turn * step) % 4) + odd
            local = (to == z) & (target_core == core)

            @pl.when(local)
            def _():
                pltpu.make_async_copy(src(to), dst, recv).start()

            @pl.when(jnp.logical_not(local))
            def _():
                remote(src(to), dst, send, recv, device(band, y_lo, to, target_core)).start()

    slot = rows(2 * (z // 2) + core, half)

    def select(i):
        chosen[i] = inter[owners[i]]

    def spread(i, odd):
        to_planes(odd, lambda to: chosen.at[i], fetched.at[i, slot], gs_sem.at[i], gr_sem.at[i])

    def arrived(odd, a):
        for step in range(4):
            source = 2 * step + odd
            wait(inter.at[2 * source + a], br_sem.at[a, source])

    def resident(odd, a):
        to_planes(odd, lambda to: inter.at[2 * to + a], res.at[a, slot], as_sem, ar_sem)

    arrived(0, 0)
    resident(0, 0)
    arrived(0, 1)
    resident(0, 1)
    arrived(1, 0)
    arrived(1, 1)
    select(0)
    spread(0, 0)
    resident(1, 0)
    resident(1, 1)
    spread(0, 1)
    for load in loads[3:]:
        load.wait()

    select(1)
    spread(1, 0)
    spread(1, 1)
    wait(res, ar_sem)

    @pl.loop(0, COUNT + 3)
    def _(step):
        @pl.when(step < COUNT)
        def _():
            i = step
            wait(fetched.at[i], gr_sem.at[i])
            shared = fetched[i]
            density = jnp.concatenate([shared * res[0], shared * res[1]], axis=1)
            lines = apply_right(density, fwd_z[...])
            lines = lines.reshape(PLANES, LEN, 2 * LEN)
            stacked = jnp.concatenate(
                [jnp.concatenate([lines[p, :, :LEN], lines[p, :, LEN:]], axis=0) for p in range(PLANES)], axis=1
            )
            field = apply_left(fwd_y[...], stacked)
            out = jnp.stack([field[:, p * LEN : (p + 1) * LEN].reshape(GROUP, 8, LEN) for p in range(PLANES)], axis=1)
            c_send[i] = out.reshape(GROUP * block, LEN)

            for target, _, theirs in others:
                remote(
                    c_send.at[i, rows(theirs, block)], c_recv.at[i, rows(place, block)],
                    cs_sem.at[i], cr_sem.at[i], target,
                ).start()

            c_recv[i, rows(place, block)] = c_send[i, rows(mine, block)]

            @pl.when(step < COUNT - 2)
            def _():
                select(step + 2)
                spread(step + 2, 0)
                spread(step + 2, 1)

        @pl.when((step >= 1) & (step < COUNT + 1))
        def _():
            i = step - 1

            @pl.when(i == 0)
            def _():
                wait(kern.at[near], kr_sem.at[0])
                wait(kern.at[far], kr_sem.at[1])

            wait(c_recv.at[i, pl.ds(0, block * (GROUP - 1))], cr_sem.at[i])
            columns = jnp.concatenate([c_recv[i, pl.ds(r, 2 * LEN, stride=4), :] for r in range(4)], axis=1)
            modes = apply_left(fwd_x[...], columns)
            scale = jnp.concatenate([kern[pl.ds(r, LEN, stride=4), :] for r in range(4)], axis=1) * (1.0 / LEN**3)
            modes = jnp.concatenate([modes[:LEN] * scale, modes[LEN:] * scale], axis=0)
            back = apply_left(inv_x[...], modes)
            for r in range(4):
                d_send[i, pl.ds(r, 2 * LEN, stride=4), :] = back[:, r * LEN : (r + 1) * LEN]

            for target, theirs, _ in others:
                remote(
                    d_send.at[i, rows(theirs, block)], d_recv.at[i, rows(mine, block)],
                    ds_sem.at[i], dr_sem.at[i], target,
                ).start()

            d_recv[i, rows(mine, block)] = d_send[i, rows(place, block)]

        @pl.when((step >= 2) & (step < COUNT + 2))
        def _():
            i = step - 2
            wait(d_recv.at[i, pl.ds(0, block * (GROUP - 1))], dr_sem.at[i])
            tiles = d_recv[i].reshape(GROUP, PLANES, 8, LEN)
            stacked = jnp.concatenate([tiles[:, p].reshape(2 * LEN, LEN) for p in range(PLANES)], axis=1)
            lines = apply_left(inv_y[...], stacked)
            flat = jnp.concatenate(
                [
                    jnp.concatenate(
                        [lines[:LEN, p * LEN : (p + 1) * LEN], lines[LEN:, p * LEN : (p + 1) * LEN]], axis=1
                    )
                    for p in range(PLANES)
                ],
                axis=0,
            )
            field = apply_right(flat, inv_z[...])
            one, two = field[:, :LEN], field[:, LEN:]
            shared = fetched[i]
            partial[i] = one * res[0] + two * res[1]

            @pl.loop(0, 2 * PLANES)
            def _(k):
                j, to_core = (z // 2 + 6 + turn * (k // 2)) % PLANES, k % 2
                to_z = 2 * j + 1 - core
                src = partial.at[i, rows(2 * j + to_core, half)]
                dst = f_recv.at[i, z]
                local = (to_z == z) & (to_core == core)

                @pl.when(local)
                def _():
                    pltpu.make_async_copy(src, dst, fr_sem.at[i]).start()

                @pl.when(jnp.logical_not(local))
                def _():
                    remote(src, dst, fs_sem.at[i], fr_sem.at[i], device(band, y_lo, to_z, to_core)).start()

            total[0] += one * shared
            total[1] += two * shared

            @pl.when(i == COUNT - 1)
            def _():
                for step_z in (2, 1, 3, 0):
                    j = (z // 2 + turn * step_z + PLANES) % PLANES
                    for a in range(2):
                        remote(
                            total.at[a, rows(j, LEN)], back_recv.at[a, rows(x, LEN)], es_sem, er_sem,
                            device(z, y_lo, 2 * j + 1 - core, y_hi),
                        ).start()

        @pl.when(step >= 3)
        def _():
            i = step - 3
            wait(f_recv.at[i], fr_sem.at[i])
            summed = f_recv[i, 0]
            for other in range(1, 8):
                summed += f_recv[i, other]
            shared_sum[i] = summed

            @pl.loop(0, 4)
            def _(k):
                to = 4 * core + k
                src = shared_sum.at[i, rows(k, yrows)]
                dst = p_recv.at[i, x]
                local = (to == band) & (y_hi == core)

                @pl.when(local)
                def _():
                    pltpu.make_async_copy(src, dst, pr_sem.at[i]).start()

                @pl.when(jnp.logical_not(local))
                def _():
                    remote(src, dst, ps_sem.at[i], pr_sem.at[i], device(to, y_lo, z, y_hi)).start()

    @pl.loop(0, COUNT)
    def _(i):
        wait(p_recv.at[i], pr_sem.at[i])
        proj[i] = p_recv[i]

    wait(back_recv, er_sem)
    exch[...] = back_recv[...]

    wait(total, es_sem)

    @pl.when(core == y_hi)
    def _():
        wait(inter.at[pl.ds(0, 14)], bs_sem)

    @pl.when(core != y_hi)
    def _():
        wait(inter, bs_sem)

    wait(kern.at[far], ks_sem.at[1])

    @pl.when(mirror != z)
    def _():
        wait(kern.at[near], ks_sem.at[0])

    @pl.when(core == 1 - z % 2)
    def _():
        wait(inter.at[pl.ds(0, 14)], as_sem)

    @pl.when(core == z % 2)
    def _():
        wait(inter, as_sem)

    @pl.loop(0, COUNT)
    def _(i):
        @pl.when(core == 1 - z % 2)
        def _():
            wait(fetched.at[i, pl.ds(0, 7 * half)], gs_sem.at[i])

        @pl.when(core == z % 2)
        def _():
            wait(fetched.at[i], gs_sem.at[i])

        wait(c_send.at[i, pl.ds(0, block * (GROUP - 1))], cs_sem.at[i])
        wait(d_send.at[i, pl.ds(0, block * (GROUP - 1))], ds_sem.at[i])

        @pl.when(core == 1 - z % 2)
        def _():
            wait(partial.at[i, pl.ds(0, ROWS - half)], fs_sem.at[i])

        @pl.when(core == z % 2)
        def _():
            wait(partial.at[i], fs_sem.at[i])

        @pl.when((core == band // 4) & (core == y_hi))
        def _():
            wait(p_recv.at[i, pl.ds(0, 3)], ps_sem.at[i])

        @pl.when((core != band // 4) | (core != y_hi))
        def _():
            wait(p_recv.at[i], ps_sem.at[i])


def shards(orbitals, owners, weights):
    vmem = pl.BlockSpec(memory_space=pltpu.VMEM)
    wide = pltpu.VMEM((COUNT, GROUP * PLANES * 8, LEN), jnp.float32)
    local = pltpu.VMEM((COUNT, ROWS, LEN), jnp.float32)
    pair = pltpu.VMEM((2, ROWS, LEN), jnp.float32)
    single = pltpu.VMEM((ROWS, LEN), jnp.float32)
    tall = pltpu.VMEM((6 * LEN, 2 * LEN), jnp.bfloat16)
    flat = pltpu.VMEM((2 * LEN, 6 * LEN), jnp.bfloat16)
    sem = pltpu.SemaphoreType.DMA
    sems = pltpu.SemaphoreType.DMA((COUNT,))
    exchange, projector = pl.pallas_call(
        kernel,
        out_shape=(
            jax.ShapeDtypeStruct((2, ROWS, LEN), jnp.float32),
            jax.ShapeDtypeStruct((COUNT, PLANES, LEN // BANDS, LEN), jnp.float32),
        ),
        in_specs=[pl.BlockSpec(memory_space=pltpu.HBM)] * 9,
        out_specs=(vmem, vmem),
        scratch_shapes=[
            pltpu.SMEM((COUNT,), jnp.int32), pair, single,
            tall, flat, flat, flat, flat, tall,
            pltpu.SemaphoreType.DMA((9,)),
            pair,
            pltpu.VMEM((2 * BANDS, LEN // 2, LEN), jnp.float32),
            pltpu.VMEM((COUNT, LEN // 2, LEN), jnp.float32),
            single, local, wide, wide, wide, wide, pair, pair, local,
            pltpu.VMEM((COUNT, 8, LEN // 2, LEN), jnp.float32),
            pltpu.VMEM((COUNT, LEN // 2, LEN), jnp.float32),
            pltpu.VMEM((COUNT, PLANES, LEN // BANDS, LEN), jnp.float32),
            pltpu.SemaphoreType.DMA((2, 8)),
            sem, sem, sem, sem((2,)), sem((2,)), sem, sem,
        ]
        + [sems] * 10,
        compiler_params=pltpu.CompilerParams(
            collective_id=0, has_side_effects=True, vmem_limit_bytes=64 * 2**20 - 2**16
        ),
        name="exchange",
    )(
        owners,
        orbitals.reshape(2, ROWS, LEN),
        weights.reshape(LEN * PLANES, LEN),
        *[jnp.asarray(table) for table in tables()],
    )
    return -exchange.reshape(2, PLANES, LEN, LEN), -projector


def solution(mesh):
    return jax.shard_map(
        shards,
        mesh=mesh,
        in_specs=(P("band", "fft", None, None), P(), P(None, "fft", None)),
        out_specs=(P("band", "fft", None, None), P(None, "fft", "band", None)),
        check_vma=False,
    )
```

```python
import functools

import jax
import jax.numpy as jnp
import ml_dtypes
import numpy as np
from jax import lax
from jax.experimental import pallas as pl
from jax.experimental.pallas import tpu as pltpu
from jax.sharding import PartitionSpec as P

MESH = pl.DeviceIdType.MESH
LEN = 128
COUNT = 4
GROUP = 32
BANDS = 8
ORDER = ((2, 2), (2, 1), (1, 2), (2, 3), (3, 2), (2, 0), (0, 2), (1, 1), (3, 3), (1, 3), (3, 1), (1, 0), (0, 1), (3, 0), (0, 3), (0, 0))
PLANES = 4
ROWS = PLANES * LEN


def halves(table):
    high = table.astype(ml_dtypes.bfloat16)
    low = (table - high.astype(np.float64)).astype(ml_dtypes.bfloat16)
    return high, low


def tables():
    n = np.arange(LEN)
    angle = 2.0 * np.pi * ((n[:, None] * n[None, :]) % LEN) / LEN
    cos, sin = np.cos(angle), np.sin(angle)
    forward = np.block([[cos, sin], [-sin, cos]])
    inverse = np.block([[cos, -sin], [sin, cos]])
    rows_y = np.arange(2 * LEN).reshape(2, GROUP, PLANES).transpose(1, 0, 2).reshape(-1)
    place, j = np.arange(GROUP)[:, None], np.arange(PLANES)[None, :]
    x, y_hi, y_lo, core = place // 8, place // 4 % 2, place // 2 % 2, place % 2
    plane = 64 * y_lo + 8 * (2 * j + 1 - core) + 4 * y_hi + x
    rows_x = np.stack([plane, plane + LEN], axis=-1).reshape(-1)

    def left(table):
        high, low = halves(table)
        return np.concatenate([high, low, high], axis=1)

    def right(table):
        high, low = halves(table)
        return np.concatenate([high, low, high], axis=0)

    return (
        right(forward.T),
        left(forward[rows_y]),
        left(forward[:, rows_x]),
        left(inverse[rows_x]),
        left(inverse[:, rows_y]),
        right(inverse.T),
    )


def parts(values):
    high = values.astype(jnp.bfloat16)
    low = (values - high.astype(jnp.float32)).astype(jnp.bfloat16)
    return high, low


def apply_left(table, values):
    high, low = parts(values)
    return jnp.dot(table, jnp.concatenate([high, high, low], axis=0), preferred_element_type=jnp.float32)


def apply_right(values, table):
    high, low = parts(values)
    return jnp.dot(jnp.concatenate([high, high, low], axis=1), table, preferred_element_type=jnp.float32)


def kernel(
    owners_in, orb_in, kern_in, fwd_z_in, fwd_y_in, fwd_x_in, inv_x_in, inv_y_in, inv_z_in,
    exch, proj,
    owners, orb, kern_own, fwd_z, fwd_y, fwd_x, inv_x, inv_y, inv_z, load_sem,
    res, inter, chosen, kern, fetched, c_send, c_recv, d_send, d_recv, total, partial, f_recv, shared_sum, br_sem,
    as_sem, ar_sem, bs_sem, ks_sem, kr_sem, es_sem, er_sem,
    gs_sem, gr_sem, cs_sem, cr_sem, ds_sem, dr_sem, fs_sem, fr_sem, ps_sem, pr_sem,
):
    band = lax.axis_index("band")
    pos = lax.axis_index("fft")
    x, y_hi = band // 2, band % 2
    y_lo, z, core = pos // 16, pos // 2 % 8, pos % 2
    half = LEN // 2
    block = PLANES * 8
    yrows = LEN // BANDS

    def device(to_band, to_y_lo, to_z, to_core):
        return (to_band, 16 * to_y_lo + 2 * to_z + to_core)

    def remote(src, dst, send, recv, target):
        return pltpu.make_async_remote_copy(
            src_ref=src, dst_ref=dst, send_sem=send, recv_sem=recv, device_id=target, device_id_type=MESH
        )

    def wait(ref, sem):
        pltpu.make_async_copy(ref, ref, sem).wait()

    def rows(index, size):
        return pl.ds(pl.multiple_of(index * size, size), size)

    def either(here, src, dst, recv, far_copy):
        @pl.when(here)
        def _():
            pltpu.make_async_copy(src, dst, recv).start()

        @pl.when(jnp.logical_not(here))
        def _():
            far_copy.start()

    loads = [
        pltpu.make_async_copy(src, dst, load_sem.at[k])
        for k, (src, dst) in enumerate(
            [(orb_in, orb), (owners_in, owners), (kern_in, kern_own), (fwd_z_in, fwd_z), (fwd_y_in, fwd_y),
             (fwd_x_in, fwd_x), (inv_x_in, inv_x), (inv_y_in, inv_y), (inv_z_in, inv_z)]
        )
    ]
    for load in loads:
        load.start()

    place = 4 * band + 2 * y_lo + core
    mine = 16 * y_lo + 2 * ((band - z + 8) % 8) + core

    barrier = pltpu.get_barrier_semaphore()

    def greet(target):
        pl.semaphore_signal(barrier, inc=1, device_id=target, device_id_type=MESH)

    def wrap(value, size):
        return jnp.where(value >= size, value - size, value)

    others = []
    step_by = jnp.where(core == 0, 1, 3)
    x_at = [x, wrap(x + step_by, 4), wrap(x + 2, 4), wrap(x + 4 - step_by, 4)]
    z_half = z // 2
    z_odd = z - 2 * z_half
    z_at = [wrap(z_half + 2, 4), wrap(z_half + 4 - step_by, 4), z_half, wrap(z_half + step_by, 4)]
    y_all = 2 * y_hi + y_lo
    y_at = []
    for value in (y_all, wrap(y_all + step_by, 4), wrap(y_all + 2, 4), wrap(y_all + 4 - step_by, 4)):
        upper = jnp.where(value >= 2, 1, 0)
        y_at.append((upper, value - 2 * upper))
    for dx, dy in ORDER:
        to_band = 2 * x_at[dx] + y_at[dy][0]
        to_y_lo = y_at[dy][1]
        to_zeta = wrap(to_band + 8 - z, 8)
        for flip in range(2):
            if (dx, dy, flip) != (0, 0, 0):
                to_core = core if flip == 0 else 1 - core
                others.append((
                    (to_band, 16 * to_y_lo + 2 * z + to_core),
                    4 * to_band + 2 * to_y_lo + to_core,
                    16 * to_y_lo + 2 * to_zeta + to_core,
                ))

    for target, _, _ in others:
        greet(target)

    @pl.loop(1, 16)
    def _(k):
        other = (2 * z + core + k) % 16
        greet((band, 16 * y_lo + other))

    greet(device((band + 4) % BANDS, y_lo, (band - z + 8) % 8, core))
    for load in loads[:3]:
        load.wait()
    total[...] = jnp.zeros_like(total)
    pl.semaphore_wait(barrier, GROUP - 1 + 15 + 1)

    for a in range(2):
        for n in (2, 1, 3, 0):
            for h in range(2):
                src = orb.at[a, rows(2 * x_at[n] + h, half)]
                dst = inter.at[2 * band + a]
                far_copy = remote(src, dst, bs_sem, br_sem.at[a, band], device(2 * x_at[n] + core, y_lo, z, h))
                if n > 0:
                    far_copy.start()
                else:
                    either((y_hi == core) & (core == h), src, dst, br_sem.at[a, band], far_copy)

    mirror = (band - z + 8) % 8
    across = (band + 4) % BANDS
    near, far = pl.ds(0, ROWS // 2), pl.ds(ROWS // 2, ROWS // 2)
    remote(
        kern_own.at[far], kern.at[far], ks_sem.at[1], kr_sem.at[1], device(across, y_lo, (across - z + 8) % 8, core)
    ).start()

    @pl.when(mirror == z)
    def _():
        pltpu.make_async_copy(kern_own.at[near], kern.at[near], kr_sem.at[0]).start()

    @pl.when(mirror != z)
    def _():
        remote(
            kern_own.at[near], kern.at[near], ks_sem.at[0], kr_sem.at[0], device(band, y_lo, mirror, core)
        ).start()

    def to_planes(odd, src, dst, send, recv):
        target_core = 1 - z_odd
        for n in range(4):
            to = 2 * z_at[n] + odd
            far_copy = remote(src(to), dst, send, recv, device(band, y_lo, to, target_core))
            if n != 2:
                far_copy.start()
            else:
                either((z_odd == odd) & (target_core == core), src(to), dst, recv, far_copy)

    slot = rows(2 * z_half + core, half)

    def select(i):
        chosen[i] = inter[owners[i]]

    def spread(i, odd):
        to_planes(odd, lambda to: chosen.at[i], fetched.at[i, slot], gs_sem.at[i], gr_sem.at[i])

    def arrived(odd, a):
        for step in range(4):
            source = 2 * step + odd
            wait(inter.at[2 * source + a], br_sem.at[a, source])

    def resident(odd, a):
        to_planes(odd, lambda to: inter.at[2 * to + a], res.at[a, slot], as_sem, ar_sem)

    arrived(0, 0)
    resident(0, 0)
    arrived(0, 1)
    resident(0, 1)
    arrived(1, 0)
    arrived(1, 1)
    select(0)
    spread(0, 0)
    resident(1, 0)
    resident(1, 1)
    spread(0, 1)
    for load in loads[3:]:
        load.wait()

    select(1)
    spread(1, 0)
    spread(1, 1)
    wait(res, ar_sem)

    @pl.loop(0, COUNT + 3)
    def _(step):
        @pl.when(step < COUNT)
        def _():
            i = step
            wait(fetched.at[i], gr_sem.at[i])
            shared = fetched[i]
            density = jnp.concatenate([shared * res[0], shared * res[1]], axis=1)
            lines = apply_right(density, fwd_z[...])
            lines = lines.reshape(PLANES, LEN, 2 * LEN)
            stacked = jnp.concatenate(
                [jnp.concatenate([lines[p, :, :LEN], lines[p, :, LEN:]], axis=0) for p in range(PLANES)], axis=1
            )
            field = apply_left(fwd_y[...], stacked)
            out = jnp.stack([field[:, p * LEN : (p + 1) * LEN].reshape(GROUP, 8, LEN) for p in range(PLANES)], axis=1)
            c_send[i] = out.reshape(GROUP * block, LEN)

            for target, _, theirs in others:
                remote(
                    c_send.at[i, rows(theirs, block)], c_recv.at[i, rows(place, block)],
                    cs_sem.at[i], cr_sem.at[i], target,
                ).start()

            c_recv[i, rows(place, block)] = c_send[i, rows(mine, block)]

            @pl.when(step < COUNT - 2)
            def _():
                select(step + 2)
                spread(step + 2, 0)
                spread(step + 2, 1)

        @pl.when((step >= 1) & (step < COUNT + 1))
        def _():
            i = step - 1

            @pl.when(i == 0)
            def _():
                wait(kern.at[near], kr_sem.at[0])
                wait(kern.at[far], kr_sem.at[1])

            wait(c_recv.at[i, pl.ds(0, block * (GROUP - 1))], cr_sem.at[i])
            columns = jnp.concatenate([c_recv[i, pl.ds(r, 2 * LEN, stride=4), :] for r in range(4)], axis=1)
            modes = apply_left(fwd_x[...], columns)
            scale = jnp.concatenate([kern[pl.ds(r, LEN, stride=4), :] for r in range(4)], axis=1) * (1.0 / LEN**3)
            modes = jnp.concatenate([modes[:LEN] * scale, modes[LEN:] * scale], axis=0)
            back = apply_left(inv_x[...], modes)
            for r in range(4):
                d_send[i, pl.ds(r, 2 * LEN, stride=4), :] = back[:, r * LEN : (r + 1) * LEN]

            for target, theirs, _ in others:
                remote(
                    d_send.at[i, rows(theirs, block)], d_recv.at[i, rows(mine, block)],
                    ds_sem.at[i], dr_sem.at[i], target,
                ).start()

            d_recv[i, rows(mine, block)] = d_send[i, rows(place, block)]

        @pl.when((step >= 2) & (step < COUNT + 2))
        def _():
            i = step - 2
            wait(d_recv.at[i, pl.ds(0, block * (GROUP - 1))], dr_sem.at[i])
            tiles = d_recv[i].reshape(GROUP, PLANES, 8, LEN)
            stacked = jnp.concatenate([tiles[:, p].reshape(2 * LEN, LEN) for p in range(PLANES)], axis=1)
            lines = apply_left(inv_y[...], stacked)
            flat = jnp.concatenate(
                [
                    jnp.concatenate(
                        [lines[:LEN, p * LEN : (p + 1) * LEN], lines[LEN:, p * LEN : (p + 1) * LEN]], axis=1
                    )
                    for p in range(PLANES)
                ],
                axis=0,
            )
            field = apply_right(flat, inv_z[...])
            one, two = field[:, :LEN], field[:, LEN:]
            shared = fetched[i]
            partial[i] = one * res[0] + two * res[1]

            for n in range(4):
                to_z = 2 * z_at[n] + 1 - core
                for to_core in range(2):
                    src = partial.at[i, rows(2 * z_at[n] + to_core, half)]
                    dst = f_recv.at[i, z]
                    far_copy = remote(src, dst, fs_sem.at[i], fr_sem.at[i], device(band, y_lo, to_z, to_core))
                    if n != 2:
                        far_copy.start()
                    else:
                        either((z_odd == 1 - core) & (core == to_core), src, dst, fr_sem.at[i], far_copy)

            total[0] += one * shared
            total[1] += two * shared

            @pl.when(i == COUNT - 1)
            def _():
                for j in z_at:
                    for a in range(2):
                        remote(
                            total.at[a, rows(j, LEN)], exch.at[a, rows(x, LEN)], es_sem, er_sem,
                            device(z, y_lo, 2 * j + 1 - core, y_hi),
                        ).start()

        @pl.when(step >= 3)
        def _():
            i = step - 3
            wait(f_recv.at[i], fr_sem.at[i])
            summed = f_recv[i, 0]
            for other in range(1, 8):
                summed += f_recv[i, other]
            shared_sum[i] = summed

            quarter = band % 4
            for k in range(4):
                part = wrap(quarter + k, 4)
                src = shared_sum.at[i, rows(part, yrows)]
                dst = proj.at[i, x]
                far_copy = remote(
                    src, dst, ps_sem.at[i], pr_sem.at[i], device(4 * core + part, y_lo, z, y_hi)
                )
                if k > 0:
                    far_copy.start()
                else:
                    either((band // 4 == core) & (y_hi == core), src, dst, pr_sem.at[i], far_copy)

    @pl.loop(0, COUNT)
    def _(i):
        wait(proj.at[i], pr_sem.at[i])

    wait(exch, er_sem)

    wait(total, es_sem)

    @pl.when(core == y_hi)
    def _():
        wait(inter.at[pl.ds(0, 14)], bs_sem)

    @pl.when(core != y_hi)
    def _():
        wait(inter, bs_sem)

    wait(kern.at[far], ks_sem.at[1])

    @pl.when(mirror != z)
    def _():
        wait(kern.at[near], ks_sem.at[0])

    @pl.when(core == 1 - z % 2)
    def _():
        wait(inter.at[pl.ds(0, 14)], as_sem)

    @pl.when(core == z % 2)
    def _():
        wait(inter, as_sem)

    @pl.loop(0, COUNT)
    def _(i):
        @pl.when(core == 1 - z % 2)
        def _():
            wait(fetched.at[i, pl.ds(0, 7 * half)], gs_sem.at[i])

        @pl.when(core == z % 2)
        def _():
            wait(fetched.at[i], gs_sem.at[i])

        wait(c_send.at[i, pl.ds(0, block * (GROUP - 1))], cs_sem.at[i])
        wait(d_send.at[i, pl.ds(0, block * (GROUP - 1))], ds_sem.at[i])

        @pl.when(core == 1 - z % 2)
        def _():
            wait(partial.at[i, pl.ds(0, ROWS - half)], fs_sem.at[i])

        @pl.when(core == z % 2)
        def _():
            wait(partial.at[i], fs_sem.at[i])

        @pl.when((core == band // 4) & (core == y_hi))
        def _():
            wait(proj.at[i, pl.ds(0, 3)], ps_sem.at[i])

        @pl.when((core != band // 4) | (core != y_hi))
        def _():
            wait(proj.at[i], ps_sem.at[i])


def negate(exchange, projector, exchange_out, projector_out):
    exchange_out[...] = -exchange[...]
    projector_out[...] = -projector[...]


def shards(orbitals, owners, weights):
    vmem = pl.BlockSpec(memory_space=pltpu.VMEM)
    wide = pltpu.VMEM((COUNT, GROUP * PLANES * 8, LEN), jnp.float32)
    local = pltpu.VMEM((COUNT, ROWS, LEN), jnp.float32)
    pair = pltpu.VMEM((2, ROWS, LEN), jnp.float32)
    single = pltpu.VMEM((ROWS, LEN), jnp.float32)
    tall = pltpu.VMEM((6 * LEN, 2 * LEN), jnp.bfloat16)
    flat = pltpu.VMEM((2 * LEN, 6 * LEN), jnp.bfloat16)
    sem = pltpu.SemaphoreType.DMA
    sems = pltpu.SemaphoreType.DMA((COUNT,))
    exchange, projector = pl.pallas_call(
        kernel,
        out_shape=(
            jax.ShapeDtypeStruct((2, ROWS, LEN), jnp.float32),
            jax.ShapeDtypeStruct((COUNT, PLANES, LEN // BANDS, LEN), jnp.float32),
        ),
        in_specs=[pl.BlockSpec(memory_space=pltpu.HBM)] * 9,
        out_specs=(pl.BlockSpec(memory_space=pltpu.HBM),) * 2,
        scratch_shapes=[
            pltpu.SMEM((COUNT,), jnp.int32), pair, single,
            tall, flat, flat, flat, flat, tall,
            pltpu.SemaphoreType.DMA((9,)),
            pair,
            pltpu.VMEM((2 * BANDS, LEN // 2, LEN), jnp.float32),
            pltpu.VMEM((COUNT, LEN // 2, LEN), jnp.float32),
            single, local, wide, wide, wide, wide, pair, local,
            pltpu.VMEM((COUNT, 8, LEN // 2, LEN), jnp.float32),
            pltpu.VMEM((COUNT, LEN // 2, LEN), jnp.float32),
            pltpu.SemaphoreType.DMA((2, 8)),
            sem, sem, sem, sem((2,)), sem((2,)), sem, sem,
        ]
        + [sems] * 10,
        compiler_params=pltpu.CompilerParams(
            collective_id=0, has_side_effects=True, vmem_limit_bytes=64 * 2**20 - 2**16
        ),
        name="exchange",
    )(
        owners,
        orbitals.reshape(2, ROWS, LEN),
        weights.reshape(LEN * PLANES, LEN),
        *[jnp.asarray(table) for table in tables()],
    )
    exchange, projector = pl.pallas_call(
        negate,
        out_shape=(
            jax.ShapeDtypeStruct((2, ROWS, LEN), jnp.float32),
            jax.ShapeDtypeStruct((COUNT, PLANES, LEN // BANDS, LEN), jnp.float32),
        ),
        in_specs=[vmem, vmem],
        out_specs=(vmem, vmem),
        name="negate",
    )(exchange, projector)
    return exchange.reshape(2, PLANES, LEN, LEN), projector


def solution(mesh):
    return jax.shard_map(
        shards,
        mesh=mesh,
        in_specs=(P("band", "fft", None, None), P(), P(None, "fft", None)),
        out_specs=(P("band", "fft", None, None), P(None, "fft", "band", None)),
        check_vma=False,
    )
```

```python
import functools

import jax
import jax.numpy as jnp
import ml_dtypes
import numpy as np
from jax import lax
from jax.experimental import pallas as pl
from jax.experimental.pallas import tpu as pltpu
from jax.sharding import PartitionSpec as P

MESH = pl.DeviceIdType.MESH
LEN = 128
COUNT = 4
GROUP = 32
BANDS = 8
ORDER = ((2, 2), (2, 1), (1, 2), (2, 3), (3, 2), (2, 0), (0, 2), (1, 1), (3, 3), (1, 3), (3, 1), (1, 0), (0, 1), (3, 0), (0, 3), (0, 0))
PLANES = 4
ROWS = PLANES * LEN


def halves(table):
    high = table.astype(ml_dtypes.bfloat16)
    low = (table - high.astype(np.float64)).astype(ml_dtypes.bfloat16)
    return high, low


def tables():
    n = np.arange(LEN)
    angle = 2.0 * np.pi * ((n[:, None] * n[None, :]) % LEN) / LEN
    cos, sin = np.cos(angle), np.sin(angle)
    forward = np.block([[cos, sin], [-sin, cos]])
    inverse = np.block([[cos, -sin], [sin, cos]])
    rows_y = np.arange(2 * LEN).reshape(2, GROUP, PLANES).transpose(1, 0, 2).reshape(-1)
    place, j = np.arange(GROUP)[:, None], np.arange(PLANES)[None, :]
    x, y_hi, y_lo, core = place // 8, place // 4 % 2, place // 2 % 2, place % 2
    plane = 64 * y_lo + 8 * (2 * j + 1 - core) + 4 * y_hi + x
    rows_x = np.stack([plane, plane + LEN], axis=-1).reshape(-1)

    def left(table):
        high, low = halves(table)
        return np.concatenate([high, low, high], axis=1)

    def right(table):
        high, low = halves(table)
        return np.concatenate([high, low, high], axis=0)

    return (
        right(forward.T),
        left(forward[rows_y]),
        left(forward[:, rows_x]),
        left(inverse[rows_x]),
        left(inverse[:, rows_y]),
        right(inverse.T),
    )


def parts(values):
    high = values.astype(jnp.bfloat16)
    low = (values - high.astype(jnp.float32)).astype(jnp.bfloat16)
    return high, low


def apply_left(table, values):
    high, low = parts(values)
    return jnp.dot(table, jnp.concatenate([high, high, low], axis=0), preferred_element_type=jnp.float32)


def apply_right(values, table):
    high, low = parts(values)
    return jnp.dot(jnp.concatenate([high, high, low], axis=1), table, preferred_element_type=jnp.float32)


def kernel(
    owners_in, orb_in, kern_in, fwd_z_in, fwd_y_in, fwd_x_in, inv_x_in, inv_y_in, inv_z_in,
    exch, proj,
    owners, orb, kern_own, fwd_z, fwd_y, fwd_x, inv_x, inv_y, inv_z, load_sem,
    res, inter, chosen, kern, fetched, c_send, c_recv, d_send, d_recv, total, partial, f_recv, shared_sum, br_sem,
    as_sem, ar_sem, bs_sem, ks_sem, kr_sem, es_sem, er_sem,
    gs_sem, gr_sem, gq_sem, cs_sem, cr_sem, ds_sem, dr_sem, fs_sem, fr_sem, ps_sem, pr_sem,
):
    band = lax.axis_index("band")
    pos = lax.axis_index("fft")
    x, y_hi = band // 2, band % 2
    y_lo, z, core = pos // 16, pos // 2 % 8, pos % 2
    half = LEN // 2
    block = PLANES * 8
    yrows = LEN // BANDS

    def device(to_band, to_y_lo, to_z, to_core):
        return (to_band, 16 * to_y_lo + 2 * to_z + to_core)

    def remote(src, dst, send, recv, target):
        return pltpu.make_async_remote_copy(
            src_ref=src, dst_ref=dst, send_sem=send, recv_sem=recv, device_id=target, device_id_type=MESH
        )

    def wait(ref, sem):
        pltpu.make_async_copy(ref, ref, sem).wait()

    def rows(index, size):
        return pl.ds(pl.multiple_of(index * size, size), size)

    def either(here, src, dst, recv, far_copy):
        @pl.when(here)
        def _():
            pltpu.make_async_copy(src, dst, recv).start()

        @pl.when(jnp.logical_not(here))
        def _():
            far_copy.start()

    loads = [
        pltpu.make_async_copy(src, dst, load_sem.at[k])
        for k, (src, dst) in enumerate(
            [(orb_in, orb), (owners_in, owners), (kern_in, kern_own), (fwd_z_in, fwd_z), (fwd_y_in, fwd_y),
             (fwd_x_in, fwd_x), (inv_x_in, inv_x), (inv_y_in, inv_y), (inv_z_in, inv_z)]
        )
    ]
    for load in loads:
        load.start()

    place = 4 * band + 2 * y_lo + core
    mine = 16 * y_lo + 2 * ((band - z + 8) % 8) + core

    barrier = pltpu.get_barrier_semaphore()

    def greet(target):
        pl.semaphore_signal(barrier, inc=1, device_id=target, device_id_type=MESH)

    def wrap(value, size):
        return jnp.where(value >= size, value - size, value)

    others = []
    step_by = jnp.where(core == 0, 1, 3)
    x_at = [x, wrap(x + step_by, 4), wrap(x + 2, 4), wrap(x + 4 - step_by, 4)]
    z_half = z // 2
    z_odd = z - 2 * z_half
    z_at = [wrap(z_half + 2, 4), wrap(z_half + 4 - step_by, 4), z_half, wrap(z_half + step_by, 4)]
    y_all = 2 * y_hi + y_lo
    y_at = []
    for value in (y_all, wrap(y_all + step_by, 4), wrap(y_all + 2, 4), wrap(y_all + 4 - step_by, 4)):
        upper = jnp.where(value >= 2, 1, 0)
        y_at.append((upper, value - 2 * upper))
    for dx, dy in ORDER:
        to_band = 2 * x_at[dx] + y_at[dy][0]
        to_y_lo = y_at[dy][1]
        to_zeta = wrap(to_band + 8 - z, 8)
        for flip in range(2):
            if (dx, dy, flip) != (0, 0, 0):
                to_core = core if flip == 0 else 1 - core
                others.append((
                    (to_band, 16 * to_y_lo + 2 * z + to_core),
                    4 * to_band + 2 * to_y_lo + to_core,
                    16 * to_y_lo + 2 * to_zeta + to_core,
                ))

    for target, _, _ in others:
        greet(target)

    @pl.loop(1, 16)
    def _(k):
        other = (2 * z + core + k) % 16
        greet((band, 16 * y_lo + other))

    greet(device((band + 4) % BANDS, y_lo, (band - z + 8) % 8, core))
    for load in loads[:3]:
        load.wait()
    total[...] = jnp.zeros_like(total)
    pl.semaphore_wait(barrier, GROUP - 1 + 15 + 1)

    for a in range(2):
        for n in (2, 1, 3, 0):
            for h in range(2):
                src = orb.at[a, rows(2 * x_at[n] + h, half)]
                dst = inter.at[2 * band + a]
                far_copy = remote(src, dst, bs_sem, br_sem.at[a, band], device(2 * x_at[n] + core, y_lo, z, h))
                if n > 0:
                    far_copy.start()
                else:
                    either((y_hi == core) & (core == h), src, dst, br_sem.at[a, band], far_copy)

    mirror = (band - z + 8) % 8
    across = (band + 4) % BANDS
    near, far = pl.ds(0, ROWS // 2), pl.ds(ROWS // 2, ROWS // 2)
    remote(
        kern_own.at[far], kern.at[far], ks_sem.at[1], kr_sem.at[1], device(across, y_lo, (across - z + 8) % 8, core)
    ).start()

    @pl.when(mirror == z)
    def _():
        pltpu.make_async_copy(kern_own.at[near], kern.at[near], kr_sem.at[0]).start()

    @pl.when(mirror != z)
    def _():
        remote(
            kern_own.at[near], kern.at[near], ks_sem.at[0], kr_sem.at[0], device(band, y_lo, mirror, core)
        ).start()

    def to_planes(odd, src, dst, send, recv):
        target_core = 1 - z_odd
        for n in range(4):
            to = 2 * z_at[n] + odd
            far_copy = remote(src(to), dst, send, recv, device(band, y_lo, to, target_core))
            if n != 2:
                far_copy.start()
            else:
                either((z_odd == odd) & (target_core == core), src(to), dst, recv, far_copy)

    slot = rows(2 * z_half + core, half)

    def select(i):
        chosen[i] = inter[owners[i]]

    relays = core == 1 - z_odd

    def spread(i):
        dst = fetched.at[i, slot]
        for step in (2, 6, 1, 7, 0):
            to = wrap(z + step, 8)
            recv = gq_sem.at[i] if step in (2, 6) else gr_sem.at[i]
            far_copy = remote(chosen.at[i], dst, gs_sem.at[i], recv, device(band, y_lo, to, 1 - z_odd))
            if step > 0:
                far_copy.start()
            else:
                either(relays, chosen.at[i], dst, recv, far_copy)

    def hand_on(i):
        @pl.when(relays)
        def _():
            wait(fetched.at[i, pl.ds(0, 4 * half)], gq_sem.at[i])
            for source, once, twice, kept in ((6, 1, 2, 0), (2, 7, 6, 1)):
                from_half = wrap(z + source, 8) // 2
                for h in (kept, 1 - kept):
                    held = fetched.at[i, rows(2 * from_half + h, half)]
                    for step in ((twice, once) if h == kept else (once,)):
                        remote(
                            held, held, gs_sem.at[i], gr_sem.at[i], device(band, y_lo, wrap(z + step, 8), core)
                        ).start()

    def fetched_here(i):
        @pl.when(relays)
        def _():
            wait(fetched.at[i, pl.ds(0, 4 * half)], gr_sem.at[i])

        @pl.when(jnp.logical_not(relays))
        def _():
            wait(fetched.at[i], gr_sem.at[i])

    def arrived(odd, a):
        for step in range(4):
            source = 2 * step + odd
            wait(inter.at[2 * source + a], br_sem.at[a, source])

    def resident(odd, a):
        to_planes(odd, lambda to: inter.at[2 * to + a], res.at[a, slot], as_sem, ar_sem)

    arrived(0, 0)
    resident(0, 0)
    arrived(0, 1)
    resident(0, 1)
    arrived(1, 0)
    arrived(1, 1)
    select(0)
    spread(0)
    resident(1, 0)
    resident(1, 1)
    for load in loads[3:]:
        load.wait()

    hand_on(0)
    select(1)
    spread(1)
    wait(res, ar_sem)

    @pl.loop(0, COUNT + 3)
    def _(step):
        @pl.when(step < COUNT)
        def _():
            i = step
            fetched_here(i)
            shared = fetched[i]
            density = jnp.concatenate([shared * res[0], shared * res[1]], axis=1)
            lines = apply_right(density, fwd_z[...])
            lines = lines.reshape(PLANES, LEN, 2 * LEN)
            stacked = jnp.concatenate(
                [jnp.concatenate([lines[p, :, :LEN], lines[p, :, LEN:]], axis=0) for p in range(PLANES)], axis=1
            )
            field = apply_left(fwd_y[...], stacked)
            out = jnp.stack([field[:, p * LEN : (p + 1) * LEN].reshape(GROUP, 8, LEN) for p in range(PLANES)], axis=1)
            c_send[i] = out.reshape(GROUP * block, LEN)

            for target, _, theirs in others:
                remote(
                    c_send.at[i, rows(theirs, block)], c_recv.at[i, rows(place, block)],
                    cs_sem.at[i], cr_sem.at[i], target,
                ).start()

            c_recv[i, rows(place, block)] = c_send[i, rows(mine, block)]

            @pl.when(step < COUNT - 1)
            def _():
                hand_on(step + 1)

            @pl.when(step < COUNT - 2)
            def _():
                select(step + 2)
                spread(step + 2)

        @pl.when((step >= 1) & (step < COUNT + 1))
        def _():
            i = step - 1

            @pl.when(i == 0)
            def _():
                wait(kern.at[near], kr_sem.at[0])
                wait(kern.at[far], kr_sem.at[1])

            wait(c_recv.at[i, pl.ds(0, block * (GROUP - 1))], cr_sem.at[i])
            columns = jnp.concatenate([c_recv[i, pl.ds(r, 2 * LEN, stride=4), :] for r in range(4)], axis=1)
            modes = apply_left(fwd_x[...], columns)
            scale = jnp.concatenate([kern[pl.ds(r, LEN, stride=4), :] for r in range(4)], axis=1) * (1.0 / LEN**3)
            modes = jnp.concatenate([modes[:LEN] * scale, modes[LEN:] * scale], axis=0)
            back = apply_left(inv_x[...], modes)
            for r in range(4):
                d_send[i, pl.ds(r, 2 * LEN, stride=4), :] = back[:, r * LEN : (r + 1) * LEN]

            for target, theirs, _ in others:
                remote(
                    d_send.at[i, rows(theirs, block)], d_recv.at[i, rows(mine, block)],
                    ds_sem.at[i], dr_sem.at[i], target,
                ).start()

            d_recv[i, rows(mine, block)] = d_send[i, rows(place, block)]

        @pl.when((step >= 2) & (step < COUNT + 2))
        def _():
            i = step - 2
            wait(d_recv.at[i, pl.ds(0, block * (GROUP - 1))], dr_sem.at[i])
            tiles = d_recv[i].reshape(GROUP, PLANES, 8, LEN)
            stacked = jnp.concatenate([tiles[:, p].reshape(2 * LEN, LEN) for p in range(PLANES)], axis=1)
            lines = apply_left(inv_y[...], stacked)
            flat = jnp.concatenate(
                [
                    jnp.concatenate(
                        [lines[:LEN, p * LEN : (p + 1) * LEN], lines[LEN:, p * LEN : (p + 1) * LEN]], axis=1
                    )
                    for p in range(PLANES)
                ],
                axis=0,
            )
            field = apply_right(flat, inv_z[...])
            one, two = field[:, :LEN], field[:, LEN:]
            shared = fetched[i]
            partial[i] = one * res[0] + two * res[1]

            for n in range(4):
                to_z = 2 * z_at[n] + 1 - core
                for to_core in range(2):
                    src = partial.at[i, rows(2 * z_at[n] + to_core, half)]
                    dst = f_recv.at[i, z]
                    far_copy = remote(src, dst, fs_sem.at[i], fr_sem.at[i], device(band, y_lo, to_z, to_core))
                    if n != 2:
                        far_copy.start()
                    else:
                        either((z_odd == 1 - core) & (core == to_core), src, dst, fr_sem.at[i], far_copy)

            total[0] += one * shared
            total[1] += two * shared

            @pl.when(i == COUNT - 1)
            def _():
                for j in z_at:
                    for a in range(2):
                        remote(
                            total.at[a, rows(j, LEN)], exch.at[a, rows(x, LEN)], es_sem, er_sem,
                            device(z, y_lo, 2 * j + 1 - core, y_hi),
                        ).start()

        @pl.when(step >= 3)
        def _():
            i = step - 3
            wait(f_recv.at[i], fr_sem.at[i])
            summed = f_recv[i, 0]
            for other in range(1, 8):
                summed += f_recv[i, other]
            shared_sum[i] = summed

            quarter = band % 4
            for k in range(4):
                part = wrap(quarter + k, 4)
                src = shared_sum.at[i, rows(part, yrows)]
                dst = proj.at[i, x]
                far_copy = remote(
                    src, dst, ps_sem.at[i], pr_sem.at[i], device(4 * core + part, y_lo, z, y_hi)
                )
                if k > 0:
                    far_copy.start()
                else:
                    either((band // 4 == core) & (y_hi == core), src, dst, pr_sem.at[i], far_copy)

    @pl.loop(0, COUNT)
    def _(i):
        wait(proj.at[i], pr_sem.at[i])

    wait(exch, er_sem)

    wait(total, es_sem)

    @pl.when(core == y_hi)
    def _():
        wait(inter.at[pl.ds(0, 14)], bs_sem)

    @pl.when(core != y_hi)
    def _():
        wait(inter, bs_sem)

    wait(kern.at[far], ks_sem.at[1])

    @pl.when(mirror != z)
    def _():
        wait(kern.at[near], ks_sem.at[0])

    @pl.when(core == 1 - z % 2)
    def _():
        wait(inter.at[pl.ds(0, 14)], as_sem)

    @pl.when(core == z % 2)
    def _():
        wait(inter, as_sem)

    @pl.loop(0, COUNT)
    def _(i):
        @pl.when(core == 1 - z % 2)
        def _():
            wait(fetched.at[i], gs_sem.at[i])
            wait(fetched.at[i, pl.ds(0, 2 * half)], gs_sem.at[i])

        @pl.when(core == z % 2)
        def _():
            wait(fetched.at[i, pl.ds(0, 5 * half)], gs_sem.at[i])

        wait(c_send.at[i, pl.ds(0, block * (GROUP - 1))], cs_sem.at[i])
        wait(d_send.at[i, pl.ds(0, block * (GROUP - 1))], ds_sem.at[i])

        @pl.when(core == 1 - z % 2)
        def _():
            wait(partial.at[i, pl.ds(0, ROWS - half)], fs_sem.at[i])

        @pl.when(core == z % 2)
        def _():
            wait(partial.at[i], fs_sem.at[i])

        @pl.when((core == band // 4) & (core == y_hi))
        def _():
            wait(proj.at[i, pl.ds(0, 3)], ps_sem.at[i])

        @pl.when((core != band // 4) | (core != y_hi))
        def _():
            wait(proj.at[i], ps_sem.at[i])


def negate(exchange, projector, exchange_out, projector_out):
    exchange_out[...] = -exchange[...]
    projector_out[...] = -projector[...]


def shards(orbitals, owners, weights):
    vmem = pl.BlockSpec(memory_space=pltpu.VMEM)
    wide = pltpu.VMEM((COUNT, GROUP * PLANES * 8, LEN), jnp.float32)
    local = pltpu.VMEM((COUNT, ROWS, LEN), jnp.float32)
    pair = pltpu.VMEM((2, ROWS, LEN), jnp.float32)
    single = pltpu.VMEM((ROWS, LEN), jnp.float32)
    tall = pltpu.VMEM((6 * LEN, 2 * LEN), jnp.bfloat16)
    flat = pltpu.VMEM((2 * LEN, 6 * LEN), jnp.bfloat16)
    sem = pltpu.SemaphoreType.DMA
    sems = pltpu.SemaphoreType.DMA((COUNT,))
    exchange, projector = pl.pallas_call(
        kernel,
        out_shape=(
            jax.ShapeDtypeStruct((2, ROWS, LEN), jnp.float32),
            jax.ShapeDtypeStruct((COUNT, PLANES, LEN // BANDS, LEN), jnp.float32),
        ),
        in_specs=[pl.BlockSpec(memory_space=pltpu.HBM)] * 9,
        out_specs=(pl.BlockSpec(memory_space=pltpu.HBM),) * 2,
        scratch_shapes=[
            pltpu.SMEM((COUNT,), jnp.int32), pair, single,
            tall, flat, flat, flat, flat, tall,
            pltpu.SemaphoreType.DMA((9,)),
            pair,
            pltpu.VMEM((2 * BANDS, LEN // 2, LEN), jnp.float32),
            pltpu.VMEM((COUNT, LEN // 2, LEN), jnp.float32),
            single, local, wide, wide, wide, wide, pair, local,
            pltpu.VMEM((COUNT, 8, LEN // 2, LEN), jnp.float32),
            pltpu.VMEM((COUNT, LEN // 2, LEN), jnp.float32),
            pltpu.SemaphoreType.DMA((2, 8)),
            sem, sem, sem, sem((2,)), sem((2,)), sem, sem,
        ]
        + [sems] * 11,
        compiler_params=pltpu.CompilerParams(
            collective_id=0, has_side_effects=True, vmem_limit_bytes=64 * 2**20 - 2**16
        ),
        name="exchange",
    )(
        owners,
        orbitals.reshape(2, ROWS, LEN),
        weights.reshape(LEN * PLANES, LEN),
        *[jnp.asarray(table) for table in tables()],
    )
    exchange, projector = pl.pallas_call(
        negate,
        out_shape=(
            jax.ShapeDtypeStruct((2, ROWS, LEN), jnp.float32),
            jax.ShapeDtypeStruct((COUNT, PLANES, LEN // BANDS, LEN), jnp.float32),
        ),
        in_specs=[vmem, vmem],
        out_specs=(vmem, vmem),
        name="negate",
    )(exchange, projector)
    return exchange.reshape(2, PLANES, LEN, LEN), projector


def solution(mesh):
    return jax.shard_map(
        shards,
        mesh=mesh,
        in_specs=(P("band", "fft", None, None), P(), P(None, "fft", None)),
        out_specs=(P("band", "fft", None, None), P(None, "fft", "band", None)),
        check_vma=False,
    )
```

```python
import functools

import jax
import jax.numpy as jnp
import ml_dtypes
import numpy as np
from jax import lax
from jax.experimental import pallas as pl
from jax.experimental.pallas import tpu as pltpu
from jax.sharding import PartitionSpec as P

MESH = pl.DeviceIdType.MESH
LEN = 128
COUNT = 4
GROUP = 32
BANDS = 8
ORDER = ((2, 2), (2, 1), (1, 2), (2, 3), (3, 2), (2, 0), (0, 2), (1, 1), (3, 3), (1, 3), (3, 1), (1, 0), (0, 1), (3, 0), (0, 3), (0, 0))
PLANES = 4
ROWS = PLANES * LEN


def halves(table):
    high = table.astype(ml_dtypes.bfloat16)
    low = (table - high.astype(np.float64)).astype(ml_dtypes.bfloat16)
    return high, low


def tables():
    n = np.arange(LEN)
    angle = 2.0 * np.pi * ((n[:, None] * n[None, :]) % LEN) / LEN
    cos, sin = np.cos(angle), np.sin(angle)
    forward = np.block([[cos, sin], [-sin, cos]])
    inverse = np.block([[cos, -sin], [sin, cos]])
    rows_y = np.arange(2 * LEN).reshape(2, GROUP, PLANES).transpose(1, 0, 2).reshape(-1)
    place, j = np.arange(GROUP)[:, None], np.arange(PLANES)[None, :]
    x, y_hi, y_lo, core = place // 8, place // 4 % 2, place // 2 % 2, place % 2
    plane = 64 * y_lo + 8 * (2 * j + 1 - core) + 4 * y_hi + x
    rows_x = np.stack([plane, plane + LEN], axis=-1).reshape(-1)

    def left(table):
        high, low = halves(table)
        return np.concatenate([high, low, high], axis=1)

    def right(table):
        high, low = halves(table)
        return np.concatenate([high, low, high], axis=0)

    return (
        right(forward.T),
        left(forward[rows_y]),
        left(forward[:, rows_x]),
        left(inverse[rows_x]),
        left(inverse[:, rows_y]),
        right(inverse.T),
    )


def parts(values):
    high = values.astype(jnp.bfloat16)
    low = (values - high.astype(jnp.float32)).astype(jnp.bfloat16)
    return high, low


def apply_left(table, values):
    high, low = parts(values)
    return jnp.dot(table, jnp.concatenate([high, high, low], axis=0), preferred_element_type=jnp.float32)


def apply_right(values, table):
    high, low = parts(values)
    return jnp.dot(jnp.concatenate([high, high, low], axis=1), table, preferred_element_type=jnp.float32)


def kernel(
    owners_in, orb_in, kern_in, fwd_z_in, fwd_y_in, fwd_x_in, inv_x_in, inv_y_in, inv_z_in,
    exch, proj,
    owners, orb, kern_own, fwd_z, fwd_y, fwd_x, inv_x, inv_y, inv_z, load_sem,
    res, inter, chosen, kern, fetched, c_send, c_recv, d_send, d_recv, total, partial, f_recv, shared_sum, br_sem,
    as_sem, ar_sem, bs_sem, ks_sem, kr_sem, es_sem, er_sem,
    gs_sem, gr_sem, gq_sem, cs_sem, cr_sem, ds_sem, dr_sem, fs_sem, fr_sem, ps_sem, pr_sem,
):
    band = lax.axis_index("band")
    pos = lax.axis_index("fft")
    x, y_hi = band // 2, band % 2
    y_lo, z, core = pos // 16, pos // 2 % 8, pos % 2
    half = LEN // 2
    block = PLANES * 8
    yrows = LEN // BANDS

    def device(to_band, to_y_lo, to_z, to_core):
        return (to_band, 16 * to_y_lo + 2 * to_z + to_core)

    def remote(src, dst, send, recv, target):
        return pltpu.make_async_remote_copy(
            src_ref=src, dst_ref=dst, send_sem=send, recv_sem=recv, device_id=target, device_id_type=MESH
        )

    def wait(ref, sem):
        pltpu.make_async_copy(ref, ref, sem).wait()

    def rows(index, size):
        return pl.ds(pl.multiple_of(index * size, size), size)

    def either(here, src, dst, recv, far_copy):
        @pl.when(here)
        def _():
            pltpu.make_async_copy(src, dst, recv).start()

        @pl.when(jnp.logical_not(here))
        def _():
            far_copy.start()

    loads = [
        pltpu.make_async_copy(src, dst, load_sem.at[k])
        for k, (src, dst) in enumerate(
            [(orb_in, orb), (owners_in, owners), (kern_in, kern_own), (fwd_z_in, fwd_z), (fwd_y_in, fwd_y),
             (fwd_x_in, fwd_x), (inv_x_in, inv_x), (inv_y_in, inv_y), (inv_z_in, inv_z)]
        )
    ]
    for load in loads:
        load.start()

    place = 4 * band + 2 * y_lo + core
    mine = 16 * y_lo + 2 * ((band - z + 8) % 8) + core

    barrier = pltpu.get_barrier_semaphore()

    def greet(target):
        pl.semaphore_signal(barrier, inc=1, device_id=target, device_id_type=MESH)

    def wrap(value, size):
        return jnp.where(value >= size, value - size, value)

    others = []
    step_by = jnp.where(core == 0, 1, 3)
    x_at = [x, wrap(x + step_by, 4), wrap(x + 2, 4), wrap(x + 4 - step_by, 4)]
    z_half = z // 2
    z_odd = z - 2 * z_half
    z_at = [wrap(z_half + 2, 4), wrap(z_half + 4 - step_by, 4), z_half, wrap(z_half + step_by, 4)]
    y_all = 2 * y_hi + y_lo
    y_at = []
    for value in (y_all, wrap(y_all + step_by, 4), wrap(y_all + 2, 4), wrap(y_all + 4 - step_by, 4)):
        upper = jnp.where(value >= 2, 1, 0)
        y_at.append((upper, value - 2 * upper))
    for dx, dy in ORDER:
        to_band = 2 * x_at[dx] + y_at[dy][0]
        to_y_lo = y_at[dy][1]
        to_zeta = wrap(to_band + 8 - z, 8)
        for flip in range(2):
            if (dx, dy, flip) != (0, 0, 0):
                to_core = core if flip == 0 else 1 - core
                others.append((
                    (to_band, 16 * to_y_lo + 2 * z + to_core),
                    4 * to_band + 2 * to_y_lo + to_core,
                    16 * to_y_lo + 2 * to_zeta + to_core,
                ))

    for target, _, _ in others:
        greet(target)

    @pl.loop(1, 16)
    def _(k):
        other = (2 * z + core + k) % 16
        greet((band, 16 * y_lo + other))

    greet(device((band + 4) % BANDS, y_lo, (band - z + 8) % 8, core))
    for load in loads[:3]:
        load.wait()
    total[...] = jnp.zeros_like(total)
    pl.semaphore_wait(barrier, GROUP - 1 + 15 + 1)

    for a in range(2):
        for n in (2, 1, 3, 0):
            for h in range(2):
                src = orb.at[a, rows(2 * x_at[n] + h, half)]
                dst = inter.at[2 * band + a]
                far_copy = remote(src, dst, bs_sem, br_sem.at[a, band], device(2 * x_at[n] + core, y_lo, z, h))
                if n > 0:
                    far_copy.start()
                else:
                    either((y_hi == core) & (core == h), src, dst, br_sem.at[a, band], far_copy)

    mirror = (band - z + 8) % 8
    across = (band + 4) % BANDS
    near, far = pl.ds(0, ROWS // 2), pl.ds(ROWS // 2, ROWS // 2)
    remote(
        kern_own.at[far], kern.at[far], ks_sem.at[1], kr_sem.at[1], device(across, y_lo, (across - z + 8) % 8, core)
    ).start()

    @pl.when(mirror == z)
    def _():
        pltpu.make_async_copy(kern_own.at[near], kern.at[near], kr_sem.at[0]).start()

    @pl.when(mirror != z)
    def _():
        remote(
            kern_own.at[near], kern.at[near], ks_sem.at[0], kr_sem.at[0], device(band, y_lo, mirror, core)
        ).start()

    def to_planes(odd, src, dst, send, recv):
        target_core = 1 - z_odd
        for n in range(4):
            to = 2 * z_at[n] + odd
            far_copy = remote(src(to), dst, send, recv, device(band, y_lo, to, target_core))
            if n != 2:
                far_copy.start()
            else:
                either((z_odd == odd) & (target_core == core), src(to), dst, recv, far_copy)

    slot = rows(2 * z_half + core, half)

    def select(i):
        chosen[i] = inter[owners[i]]

    relays = core == 1 - z_odd

    def spread(i):
        dst = fetched.at[i, slot]
        for step in (2, 6, 1, 7, 0):
            to = wrap(z + step, 8)
            recv = gq_sem.at[i] if step in (2, 6) else gr_sem.at[i]
            far_copy = remote(chosen.at[i], dst, gs_sem.at[i], recv, device(band, y_lo, to, 1 - z_odd))
            if step > 0:
                far_copy.start()
            else:
                either(relays, chosen.at[i], dst, recv, far_copy)

    def hand_on(i):
        @pl.when(relays)
        def _():
            wait(fetched.at[i, pl.ds(0, 4 * half)], gq_sem.at[i])
            for source, once, twice, kept in ((6, 1, 2, 0), (2, 7, 6, 1)):
                from_half = wrap(z + source, 8) // 2
                for h in (kept, 1 - kept):
                    held = fetched.at[i, rows(2 * from_half + h, half)]
                    for step in ((twice, once) if h == kept else (once,)):
                        remote(
                            held, held, gs_sem.at[i], gr_sem.at[i], device(band, y_lo, wrap(z + step, 8), core)
                        ).start()

    def fetched_here(i):
        @pl.when(relays)
        def _():
            wait(fetched.at[i, pl.ds(0, 4 * half)], gr_sem.at[i])

        @pl.when(jnp.logical_not(relays))
        def _():
            wait(fetched.at[i], gr_sem.at[i])

    def arrived(odd, a):
        for step in range(4):
            source = 2 * step + odd
            wait(inter.at[2 * source + a], br_sem.at[a, source])

    def resident(odd, a):
        to_planes(odd, lambda to: inter.at[2 * to + a], res.at[a, slot], as_sem, ar_sem)

    arrived(0, 0)
    resident(0, 0)
    arrived(0, 1)
    resident(0, 1)
    arrived(1, 0)
    arrived(1, 1)
    select(0)
    spread(0)
    resident(1, 0)
    resident(1, 1)
    for load in loads[3:]:
        load.wait()

    hand_on(0)
    wait(res, ar_sem)
    select(1)
    spread(1)

    @pl.loop(0, COUNT + 3)
    def _(step):
        @pl.when(step < COUNT)
        def _():
            i = step
            fetched_here(i)
            shared = fetched[i]
            density = jnp.concatenate([shared * res[0], shared * res[1]], axis=1)
            lines = apply_right(density, fwd_z[...])
            lines = lines.reshape(PLANES, LEN, 2 * LEN)
            stacked = jnp.concatenate(
                [jnp.concatenate([lines[p, :, :LEN], lines[p, :, LEN:]], axis=0) for p in range(PLANES)], axis=1
            )
            field = apply_left(fwd_y[...], stacked)
            out = jnp.stack([field[:, p * LEN : (p + 1) * LEN].reshape(GROUP, 8, LEN) for p in range(PLANES)], axis=1)
            c_send[i] = out.reshape(GROUP * block, LEN)

            for target, _, theirs in others:
                remote(
                    c_send.at[i, rows(theirs, block)], c_recv.at[i, rows(place, block)],
                    cs_sem.at[i], cr_sem.at[i], target,
                ).start()

            c_recv[i, rows(place, block)] = c_send[i, rows(mine, block)]

            @pl.when(step < COUNT - 1)
            def _():
                hand_on(step + 1)

            @pl.when(step < COUNT - 2)
            def _():
                select(step + 2)
                spread(step + 2)

        @pl.when((step >= 1) & (step < COUNT + 1))
        def _():
            i = step - 1

            @pl.when(i == 0)
            def _():
                wait(kern.at[near], kr_sem.at[0])
                wait(kern.at[far], kr_sem.at[1])

            wait(c_recv.at[i, pl.ds(0, block * (GROUP - 1))], cr_sem.at[i])
            columns = jnp.concatenate([c_recv[i, pl.ds(r, 2 * LEN, stride=4), :] for r in range(4)], axis=1)
            modes = apply_left(fwd_x[...], columns)
            scale = jnp.concatenate([kern[pl.ds(r, LEN, stride=4), :] for r in range(4)], axis=1) * (1.0 / LEN**3)
            modes = jnp.concatenate([modes[:LEN] * scale, modes[LEN:] * scale], axis=0)
            back = apply_left(inv_x[...], modes)
            for r in range(4):
                d_send[i, pl.ds(r, 2 * LEN, stride=4), :] = back[:, r * LEN : (r + 1) * LEN]

            for target, theirs, _ in others:
                remote(
                    d_send.at[i, rows(theirs, block)], d_recv.at[i, rows(mine, block)],
                    ds_sem.at[i], dr_sem.at[i], target,
                ).start()

            d_recv[i, rows(mine, block)] = d_send[i, rows(place, block)]

        @pl.when((step >= 2) & (step < COUNT + 2))
        def _():
            i = step - 2
            wait(d_recv.at[i, pl.ds(0, block * (GROUP - 1))], dr_sem.at[i])
            tiles = d_recv[i].reshape(GROUP, PLANES, 8, LEN)
            stacked = jnp.concatenate([tiles[:, p].reshape(2 * LEN, LEN) for p in range(PLANES)], axis=1)
            lines = apply_left(inv_y[...], stacked)
            flat = jnp.concatenate(
                [
                    jnp.concatenate(
                        [lines[:LEN, p * LEN : (p + 1) * LEN], lines[LEN:, p * LEN : (p + 1) * LEN]], axis=1
                    )
                    for p in range(PLANES)
                ],
                axis=0,
            )
            field = apply_right(flat, inv_z[...])
            one, two = field[:, :LEN], field[:, LEN:]
            shared = fetched[i]
            partial[i] = one * res[0] + two * res[1]

            for n in range(4):
                to_z = 2 * z_at[n] + 1 - core
                for to_core in range(2):
                    src = partial.at[i, rows(2 * z_at[n] + to_core, half)]
                    dst = f_recv.at[i, z]
                    far_copy = remote(src, dst, fs_sem.at[i], fr_sem.at[i], device(band, y_lo, to_z, to_core))
                    if n != 2:
                        far_copy.start()
                    else:
                        either((z_odd == 1 - core) & (core == to_core), src, dst, fr_sem.at[i], far_copy)

            total[0] += one * shared
            total[1] += two * shared

            @pl.when(i == COUNT - 1)
            def _():
                for j in z_at:
                    for a in range(2):
                        remote(
                            total.at[a, rows(j, LEN)], exch.at[a, rows(x, LEN)], es_sem, er_sem,
                            device(z, y_lo, 2 * j + 1 - core, y_hi),
                        ).start()

        @pl.when(step >= 3)
        def _():
            i = step - 3
            wait(f_recv.at[i], fr_sem.at[i])
            summed = f_recv[i, 0]
            for other in range(1, 8):
                summed += f_recv[i, other]
            shared_sum[i] = summed

            quarter = band % 4
            for k in range(4):
                part = wrap(quarter + k, 4)
                src = shared_sum.at[i, rows(part, yrows)]
                dst = proj.at[i, x]
                far_copy = remote(
                    src, dst, ps_sem.at[i], pr_sem.at[i], device(4 * core + part, y_lo, z, y_hi)
                )
                if k > 0:
                    far_copy.start()
                else:
                    either((band // 4 == core) & (y_hi == core), src, dst, pr_sem.at[i], far_copy)

    @pl.loop(0, COUNT)
    def _(i):
        wait(proj.at[i], pr_sem.at[i])

    wait(exch, er_sem)

    wait(total, es_sem)

    @pl.when(core == y_hi)
    def _():
        wait(inter.at[pl.ds(0, 14)], bs_sem)

    @pl.when(core != y_hi)
    def _():
        wait(inter, bs_sem)

    wait(kern.at[far], ks_sem.at[1])

    @pl.when(mirror != z)
    def _():
        wait(kern.at[near], ks_sem.at[0])

    @pl.when(core == 1 - z % 2)
    def _():
        wait(inter.at[pl.ds(0, 14)], as_sem)

    @pl.when(core == z % 2)
    def _():
        wait(inter, as_sem)

    @pl.loop(0, COUNT)
    def _(i):
        @pl.when(core == 1 - z % 2)
        def _():
            wait(fetched.at[i], gs_sem.at[i])
            wait(fetched.at[i, pl.ds(0, 2 * half)], gs_sem.at[i])

        @pl.when(core == z % 2)
        def _():
            wait(fetched.at[i, pl.ds(0, 5 * half)], gs_sem.at[i])

        wait(c_send.at[i, pl.ds(0, block * (GROUP - 1))], cs_sem.at[i])
        wait(d_send.at[i, pl.ds(0, block * (GROUP - 1))], ds_sem.at[i])

        @pl.when(core == 1 - z % 2)
        def _():
            wait(partial.at[i, pl.ds(0, ROWS - half)], fs_sem.at[i])

        @pl.when(core == z % 2)
        def _():
            wait(partial.at[i], fs_sem.at[i])

        @pl.when((core == band // 4) & (core == y_hi))
        def _():
            wait(proj.at[i, pl.ds(0, 3)], ps_sem.at[i])

        @pl.when((core != band // 4) | (core != y_hi))
        def _():
            wait(proj.at[i], ps_sem.at[i])


def negate(exchange, projector, exchange_out, projector_out):
    exchange_out[...] = -exchange[...]
    projector_out[...] = -projector[...]


def shards(orbitals, owners, weights):
    vmem = pl.BlockSpec(memory_space=pltpu.VMEM)
    wide = pltpu.VMEM((COUNT, GROUP * PLANES * 8, LEN), jnp.float32)
    local = pltpu.VMEM((COUNT, ROWS, LEN), jnp.float32)
    pair = pltpu.VMEM((2, ROWS, LEN), jnp.float32)
    single = pltpu.VMEM((ROWS, LEN), jnp.float32)
    tall = pltpu.VMEM((6 * LEN, 2 * LEN), jnp.bfloat16)
    flat = pltpu.VMEM((2 * LEN, 6 * LEN), jnp.bfloat16)
    sem = pltpu.SemaphoreType.DMA
    sems = pltpu.SemaphoreType.DMA((COUNT,))
    exchange, projector = pl.pallas_call(
        kernel,
        out_shape=(
            jax.ShapeDtypeStruct((2, ROWS, LEN), jnp.float32),
            jax.ShapeDtypeStruct((COUNT, PLANES, LEN // BANDS, LEN), jnp.float32),
        ),
        in_specs=[pl.BlockSpec(memory_space=pltpu.HBM)] * 9,
        out_specs=(pl.BlockSpec(memory_space=pltpu.HBM),) * 2,
        scratch_shapes=[
            pltpu.SMEM((COUNT,), jnp.int32), pair, single,
            tall, flat, flat, flat, flat, tall,
            pltpu.SemaphoreType.DMA((9,)),
            pair,
            pltpu.VMEM((2 * BANDS, LEN // 2, LEN), jnp.float32),
            pltpu.VMEM((COUNT, LEN // 2, LEN), jnp.float32),
            single, local, wide, wide, wide, wide, pair, local,
            pltpu.VMEM((COUNT, 8, LEN // 2, LEN), jnp.float32),
            pltpu.VMEM((COUNT, LEN // 2, LEN), jnp.float32),
            pltpu.SemaphoreType.DMA((2, 8)),
            sem, sem, sem, sem((2,)), sem((2,)), sem, sem,
        ]
        + [sems] * 11,
        compiler_params=pltpu.CompilerParams(
            collective_id=0, has_side_effects=True, vmem_limit_bytes=64 * 2**20 - 2**16
        ),
        name="exchange",
    )(
        owners,
        orbitals.reshape(2, ROWS, LEN),
        weights.reshape(LEN * PLANES, LEN),
        *[jnp.asarray(table) for table in tables()],
    )
    exchange, projector = pl.pallas_call(
        negate,
        out_shape=(
            jax.ShapeDtypeStruct((2, ROWS, LEN), jnp.float32),
            jax.ShapeDtypeStruct((COUNT, PLANES, LEN // BANDS, LEN), jnp.float32),
        ),
        in_specs=[vmem, vmem],
        out_specs=(vmem, vmem),
        name="negate",
    )(exchange, projector)
    return exchange.reshape(2, PLANES, LEN, LEN), projector


def solution(mesh):
    return jax.shard_map(
        shards,
        mesh=mesh,
        in_specs=(P("band", "fft", None, None), P(), P(None, "fft", None)),
        out_specs=(P("band", "fft", None, None), P(None, "fft", "band", None)),
        check_vma=False,
    )
```

```python
import functools

import jax
import jax.numpy as jnp
import ml_dtypes
import numpy as np
from jax import lax
from jax.experimental import pallas as pl
from jax.experimental.pallas import tpu as pltpu
from jax.sharding import PartitionSpec as P

MESH = pl.DeviceIdType.MESH
LEN = 128
COUNT = 4
GROUP = 32
BANDS = 8
ORDER = ((2, 2), (2, 1), (1, 2), (2, 3), (3, 2), (2, 0), (0, 2), (1, 1), (3, 3), (1, 3), (3, 1), (1, 0), (0, 1), (3, 0), (0, 3), (0, 0))
PLANES = 4
ROWS = PLANES * LEN


def halves(table):
    high = table.astype(ml_dtypes.bfloat16)
    low = (table - high.astype(np.float64)).astype(ml_dtypes.bfloat16)
    return high, low


def tables():
    n = np.arange(LEN)
    angle = 2.0 * np.pi * ((n[:, None] * n[None, :]) % LEN) / LEN
    cos, sin = np.cos(angle), np.sin(angle)
    forward = np.block([[cos, sin], [-sin, cos]])
    inverse = np.block([[cos, -sin], [sin, cos]])
    rows_y = np.arange(2 * LEN).reshape(2, GROUP, PLANES).transpose(1, 0, 2).reshape(-1)
    place, j = np.arange(GROUP)[:, None], np.arange(PLANES)[None, :]
    x, y_hi, y_lo, core = place // 8, place // 4 % 2, place // 2 % 2, place % 2
    plane = 64 * y_lo + 8 * (2 * j + 1 - core) + 4 * y_hi + x
    rows_x = np.stack([plane, plane + LEN], axis=-1).reshape(-1)

    def left(table):
        high, low = halves(table)
        return np.concatenate([high, low, high], axis=1)

    def right(table):
        high, low = halves(table)
        return np.concatenate([high, low, high], axis=0)

    return (
        right(forward.T),
        left(forward[rows_y]),
        left(forward[:, rows_x]),
        left(inverse[rows_x]),
        left(inverse[:, rows_y]),
        right(inverse.T),
    )


def parts(values):
    high = values.astype(jnp.bfloat16)
    low = (values - high.astype(jnp.float32)).astype(jnp.bfloat16)
    return high, low


def apply_left(table, values):
    high, low = parts(values)
    return jnp.dot(table, jnp.concatenate([high, high, low], axis=0), preferred_element_type=jnp.float32)


def apply_right(values, table):
    high, low = parts(values)
    return jnp.dot(jnp.concatenate([high, high, low], axis=1), table, preferred_element_type=jnp.float32)


def kernel(
    owners_in, orb_in, kern_in, fwd_z_in, fwd_y_in, fwd_x_in, inv_x_in, inv_y_in, inv_z_in,
    exch, proj,
    owners, orb, kern_own, fwd_z, fwd_y, fwd_x, inv_x, inv_y, inv_z, load_sem,
    res, inter, chosen, kern, fetched, c_send, c_recv, d_send, d_recv, total, partial, f_recv, shared_sum, br_sem,
    as_sem, ar_sem, bs_sem, ks_sem, kr_sem, es_sem, er_sem,
    gs_sem, gr_sem, gq_sem, cs_sem, cr_sem, ds_sem, dr_sem, fs_sem, fr_sem, ps_sem, pr_sem,
):
    band = lax.axis_index("band")
    pos = lax.axis_index("fft")
    x, y_hi = band // 2, band % 2
    y_lo, z, core = pos // 16, pos // 2 % 8, pos % 2
    half = LEN // 2
    block = PLANES * 8
    yrows = LEN // BANDS

    def device(to_band, to_y_lo, to_z, to_core):
        return (to_band, 16 * to_y_lo + 2 * to_z + to_core)

    def remote(src, dst, send, recv, target):
        return pltpu.make_async_remote_copy(
            src_ref=src, dst_ref=dst, send_sem=send, recv_sem=recv, device_id=target, device_id_type=MESH
        )

    def wait(ref, sem):
        pltpu.make_async_copy(ref, ref, sem).wait()

    def rows(index, size):
        return pl.ds(pl.multiple_of(index * size, size), size)

    def either(here, src, dst, recv, far_copy):
        @pl.when(here)
        def _():
            pltpu.make_async_copy(src, dst, recv).start()

        @pl.when(jnp.logical_not(here))
        def _():
            far_copy.start()

    loads = [
        pltpu.make_async_copy(src, dst, load_sem.at[k])
        for k, (src, dst) in enumerate(
            [(orb_in, orb), (owners_in, owners), (kern_in, kern_own), (fwd_z_in, fwd_z), (fwd_y_in, fwd_y),
             (fwd_x_in, fwd_x), (inv_x_in, inv_x), (inv_y_in, inv_y), (inv_z_in, inv_z)]
        )
    ]
    for load in loads:
        load.start()

    place = 4 * band + 2 * y_lo + core
    mine = 16 * y_lo + 2 * ((band - z + 8) % 8) + core

    barrier = pltpu.get_barrier_semaphore()

    def greet(target):
        pl.semaphore_signal(barrier, inc=1, device_id=target, device_id_type=MESH)

    def wrap(value, size):
        return jnp.where(value >= size, value - size, value)

    others = []
    step_by = jnp.where(core == 0, 1, 3)
    x_at = [x, wrap(x + step_by, 4), wrap(x + 2, 4), wrap(x + 4 - step_by, 4)]
    z_half = z // 2
    z_odd = z - 2 * z_half
    z_at = [wrap(z_half + 2, 4), wrap(z_half + 4 - step_by, 4), z_half, wrap(z_half + step_by, 4)]
    y_all = 2 * y_hi + y_lo
    y_at = []
    for value in (y_all, wrap(y_all + step_by, 4), wrap(y_all + 2, 4), wrap(y_all + 4 - step_by, 4)):
        upper = jnp.where(value >= 2, 1, 0)
        y_at.append((upper, value - 2 * upper))
    for dx, dy in ORDER:
        to_band = 2 * x_at[dx] + y_at[dy][0]
        to_y_lo = y_at[dy][1]
        to_zeta = wrap(to_band + 8 - z, 8)
        for flip in range(2):
            if (dx, dy, flip) != (0, 0, 0):
                to_core = core if flip == 0 else 1 - core
                others.append((
                    (to_band, 16 * to_y_lo + 2 * z + to_core),
                    4 * to_band + 2 * to_y_lo + to_core,
                    16 * to_y_lo + 2 * to_zeta + to_core,
                ))

    for target, _, _ in others:
        greet(target)

    @pl.loop(1, 16)
    def _(k):
        other = (2 * z + core + k) % 16
        greet((band, 16 * y_lo + other))

    greet(device((band + 4) % BANDS, y_lo, (band - z + 8) % 8, core))
    for load in loads[:3]:
        load.wait()
    total[...] = jnp.zeros_like(total)
    pl.semaphore_wait(barrier, GROUP - 1 + 15 + 1)

    for a in range(2):
        for n in (2, 1, 3, 0):
            for h in range(2):
                src = orb.at[a, rows(2 * x_at[n] + h, half)]
                dst = inter.at[2 * band + a]
                far_copy = remote(src, dst, bs_sem, br_sem.at[a, band], device(2 * x_at[n] + core, y_lo, z, h))
                if n > 0:
                    far_copy.start()
                else:
                    either((y_hi == core) & (core == h), src, dst, br_sem.at[a, band], far_copy)

    mirror = (band - z + 8) % 8
    across = (band + 4) % BANDS
    near, far = pl.ds(0, ROWS // 2), pl.ds(ROWS // 2, ROWS // 2)
    remote(
        kern_own.at[far], kern.at[far], ks_sem.at[1], kr_sem.at[1], device(across, y_lo, (across - z + 8) % 8, core)
    ).start()

    @pl.when(mirror == z)
    def _():
        pltpu.make_async_copy(kern_own.at[near], kern.at[near], kr_sem.at[0]).start()

    @pl.when(mirror != z)
    def _():
        remote(
            kern_own.at[near], kern.at[near], ks_sem.at[0], kr_sem.at[0], device(band, y_lo, mirror, core)
        ).start()

    def to_planes(odd, src, dst, send, recv):
        target_core = 1 - z_odd
        for n in range(4):
            to = 2 * z_at[n] + odd
            far_copy = remote(src(to), dst, send, recv, device(band, y_lo, to, target_core))
            if n != 2:
                far_copy.start()
            else:
                either((z_odd == odd) & (target_core == core), src(to), dst, recv, far_copy)

    slot = rows(2 * z_half + core, half)

    def select(i):
        chosen[i] = inter[owners[i]]

    relays = core == 1 - z_odd

    def spread(i):
        dst = fetched.at[i, slot]
        for step in (2, 6, 1, 7, 0):
            to = wrap(z + step, 8)
            recv = gq_sem.at[i] if step in (2, 6) else gr_sem.at[i]
            far_copy = remote(chosen.at[i], dst, gs_sem.at[i], recv, device(band, y_lo, to, 1 - z_odd))
            if step > 0:
                far_copy.start()
            else:
                either(relays, chosen.at[i], dst, recv, far_copy)

    def hand_on(i):
        @pl.when(relays)
        def _():
            wait(fetched.at[i, pl.ds(0, 4 * half)], gq_sem.at[i])
            for source, once, twice, kept in ((6, 1, 2, 0), (2, 7, 6, 1)):
                from_half = wrap(z + source, 8) // 2
                for h in (kept, 1 - kept):
                    held = fetched.at[i, rows(2 * from_half + h, half)]
                    for step in ((twice, once) if h == kept else (once,)):
                        remote(
                            held, held, gs_sem.at[i], gr_sem.at[i], device(band, y_lo, wrap(z + step, 8), core)
                        ).start()

    def fetched_here(i):
        @pl.when(relays)
        def _():
            wait(fetched.at[i, pl.ds(0, 4 * half)], gr_sem.at[i])

        @pl.when(jnp.logical_not(relays))
        def _():
            wait(fetched.at[i], gr_sem.at[i])

    def arrived(odd, a):
        for step in range(4):
            source = 2 * step + odd
            wait(inter.at[2 * source + a], br_sem.at[a, source])

    def resident(odd, a):
        to_planes(odd, lambda to: inter.at[2 * to + a], res.at[a, slot], as_sem, ar_sem)

    arrived(0, 0)
    resident(0, 0)
    arrived(0, 1)
    resident(0, 1)
    arrived(1, 0)
    arrived(1, 1)
    select(0)
    spread(0)
    resident(1, 0)
    resident(1, 1)
    for load in loads[3:]:
        load.wait()

    hand_on(0)
    wait(res, ar_sem)
    select(1)
    spread(1)

    @pl.loop(0, COUNT + 3)
    def _(step):
        @pl.when(step < COUNT)
        def _():
            i = step
            fetched_here(i)
            shared = fetched[i]
            density = jnp.concatenate([shared * res[0], shared * res[1]], axis=1)
            lines = apply_right(density, fwd_z[...])
            lines = lines.reshape(PLANES, LEN, 2 * LEN)
            stacked = jnp.concatenate(
                [jnp.concatenate([lines[p, :, :LEN], lines[p, :, LEN:]], axis=0) for p in range(PLANES)], axis=1
            )
            field = apply_left(fwd_y[...], stacked)
            out = jnp.stack([field[:, p * LEN : (p + 1) * LEN].reshape(GROUP, 8, LEN) for p in range(PLANES)], axis=1)
            c_send[i] = out.reshape(GROUP * block, LEN)

            for target, _, theirs in others:
                remote(
                    c_send.at[i, rows(theirs, block)], c_recv.at[i, rows(place, block)],
                    cs_sem.at[i], cr_sem.at[i], target,
                ).start()

            c_recv[i, rows(place, block)] = c_send[i, rows(mine, block)]

            @pl.when(step < COUNT - 1)
            def _():
                hand_on(step + 1)

            @pl.when(step < COUNT - 2)
            def _():
                select(step + 2)
                spread(step + 2)

        @pl.when((step >= 1) & (step < COUNT + 1))
        def _():
            i = step - 1

            @pl.when(i == 0)
            def _():
                wait(kern.at[near], kr_sem.at[0])
                wait(kern.at[far], kr_sem.at[1])

            wait(c_recv.at[i, pl.ds(0, block * (GROUP - 1))], cr_sem.at[i])
            columns = jnp.concatenate([c_recv[i, pl.ds(r, 2 * LEN, stride=4), :] for r in range(4)], axis=1)
            modes = apply_left(fwd_x[...], columns)
            scale = jnp.concatenate([kern[pl.ds(r, LEN, stride=4), :] for r in range(4)], axis=1) * (1.0 / LEN**3)
            modes = jnp.concatenate([modes[:LEN] * scale, modes[LEN:] * scale], axis=0)
            back = apply_left(inv_x[...], modes)
            for r in range(4):
                d_send[i, pl.ds(r, 2 * LEN, stride=4), :] = back[:, r * LEN : (r + 1) * LEN]

            for target, theirs, _ in others:
                remote(
                    d_send.at[i, rows(theirs, block)], d_recv.at[i, rows(mine, block)],
                    ds_sem.at[i], dr_sem.at[i], target,
                ).start()

            d_recv[i, rows(mine, block)] = d_send[i, rows(place, block)]

        @pl.when((step >= 2) & (step < COUNT + 2))
        def _():
            i = step - 2
            wait(d_recv.at[i, pl.ds(0, block * (GROUP - 1))], dr_sem.at[i])
            tiles = d_recv[i].reshape(GROUP, PLANES, 8, LEN)
            stacked = jnp.concatenate([tiles[:, p].reshape(2 * LEN, LEN) for p in range(PLANES)], axis=1)
            lines = apply_left(inv_y[...], stacked)
            flat = jnp.concatenate(
                [
                    jnp.concatenate(
                        [lines[:LEN, p * LEN : (p + 1) * LEN], lines[LEN:, p * LEN : (p + 1) * LEN]], axis=1
                    )
                    for p in range(PLANES)
                ],
                axis=0,
            )
            field = apply_right(flat, inv_z[...])
            one, two = field[:, :LEN], field[:, LEN:]
            shared = fetched[i]
            partial[i] = one * res[0] + two * res[1]

            for n in range(4):
                to_z = 2 * z_at[n] + 1 - core
                for to_core in range(2):
                    src = partial.at[i, rows(2 * z_at[n] + to_core, half)]
                    dst = f_recv.at[i, z]
                    far_copy = remote(src, dst, fs_sem.at[i], fr_sem.at[i], device(band, y_lo, to_z, to_core))
                    if n != 2:
                        far_copy.start()
                    else:
                        either((z_odd == 1 - core) & (core == to_core), src, dst, fr_sem.at[i], far_copy)

            total[0] += one * shared
            total[1] += two * shared

            @pl.when(i == COUNT - 1)
            def _():
                for j in z_at:
                    for a in range(2):
                        remote(
                            total.at[a, rows(j, LEN)], exch.at[a, rows(x, LEN)], es_sem, er_sem,
                            device(z, y_lo, 2 * j + 1 - core, y_hi),
                        ).start()

        @pl.when(step >= 3)
        def _():
            i = step - 3
            wait(f_recv.at[i], fr_sem.at[i])
            summed = f_recv[i, 0]
            for other in range(1, 8):
                summed += f_recv[i, other]
            shared_sum[i] = summed

            quarter = band % 4
            for k in range(4):
                part = wrap(quarter + k, 4)
                src = shared_sum.at[i, rows(part, yrows)]
                dst = proj.at[i, x]
                far_copy = remote(
                    src, dst, ps_sem.at[i], pr_sem.at[i], device(4 * core + part, y_lo, z, y_hi)
                )
                if k > 0:
                    far_copy.start()
                else:
                    either((band // 4 == core) & (y_hi == core), src, dst, pr_sem.at[i], far_copy)

    @pl.loop(0, COUNT)
    def _(i):
        wait(proj.at[i], pr_sem.at[i])

    wait(exch, er_sem)

    wait(total, es_sem)

    @pl.when(core == y_hi)
    def _():
        wait(inter.at[pl.ds(0, 14)], bs_sem)

    @pl.when(core != y_hi)
    def _():
        wait(inter, bs_sem)

    wait(kern.at[far], ks_sem.at[1])

    @pl.when(mirror != z)
    def _():
        wait(kern.at[near], ks_sem.at[0])

    @pl.when(core == 1 - z % 2)
    def _():
        wait(inter.at[pl.ds(0, 14)], as_sem)

    @pl.when(core == z % 2)
    def _():
        wait(inter, as_sem)

    @pl.loop(0, COUNT)
    def _(i):
        @pl.when(core == 1 - z % 2)
        def _():
            wait(fetched.at[i], gs_sem.at[i])
            wait(fetched.at[i, pl.ds(0, 2 * half)], gs_sem.at[i])

        @pl.when(core == z % 2)
        def _():
            wait(fetched.at[i, pl.ds(0, 5 * half)], gs_sem.at[i])

        wait(c_send.at[i, pl.ds(0, block * (GROUP - 1))], cs_sem.at[i])
        wait(d_send.at[i, pl.ds(0, block * (GROUP - 1))], ds_sem.at[i])

        @pl.when(core == 1 - z % 2)
        def _():
            wait(partial.at[i, pl.ds(0, ROWS - half)], fs_sem.at[i])

        @pl.when(core == z % 2)
        def _():
            wait(partial.at[i], fs_sem.at[i])

        @pl.when((core == band // 4) & (core == y_hi))
        def _():
            wait(proj.at[i, pl.ds(0, 3)], ps_sem.at[i])

        @pl.when((core != band // 4) | (core != y_hi))
        def _():
            wait(proj.at[i], ps_sem.at[i])


def negate(exchange, projector, exchange_out, projector_out):
    exchange_out[...] = -exchange[...]
    projector_out[...] = -projector[...]


def shards(orbitals, owners, weights):
    vmem = pl.BlockSpec(memory_space=pltpu.VMEM)
    wide = pltpu.VMEM((COUNT, GROUP * PLANES * 8, LEN), jnp.float32)
    local = pltpu.VMEM((COUNT, ROWS, LEN), jnp.float32)
    pair = pltpu.VMEM((2, ROWS, LEN), jnp.float32)
    single = pltpu.VMEM((ROWS, LEN), jnp.float32)
    spare = pltpu.VMEM((ROWS + 8, LEN), jnp.float32)
    wide_spare = pltpu.VMEM((COUNT, GROUP * PLANES * 8 + 8, LEN), jnp.float32)
    tall = pltpu.VMEM((6 * LEN, 2 * LEN), jnp.bfloat16)
    flat = pltpu.VMEM((2 * LEN, 6 * LEN), jnp.bfloat16)
    sem = pltpu.SemaphoreType.DMA
    sems = pltpu.SemaphoreType.DMA((COUNT,))
    exchange, projector = pl.pallas_call(
        kernel,
        out_shape=(
            jax.ShapeDtypeStruct((2, ROWS, LEN), jnp.float32),
            jax.ShapeDtypeStruct((COUNT, PLANES, LEN // BANDS, LEN), jnp.float32),
        ),
        in_specs=[pl.BlockSpec(memory_space=pltpu.HBM)] * 9,
        out_specs=(pl.BlockSpec(memory_space=pltpu.HBM),) * 2,
        scratch_shapes=[
            pltpu.SMEM((COUNT,), jnp.int32), pair, single,
            tall, flat, flat, flat, flat, tall,
            pltpu.SemaphoreType.DMA((9,)),
            pair,
            pltpu.VMEM((2 * BANDS, LEN // 2, LEN), jnp.float32),
            pltpu.VMEM((COUNT, LEN // 2, LEN), jnp.float32),
            spare, local, wide, wide_spare, wide_spare, wide, pair, local,
            pltpu.VMEM((COUNT, 8, LEN // 2, LEN), jnp.float32),
            pltpu.VMEM((COUNT, LEN // 2, LEN), jnp.float32),
            pltpu.SemaphoreType.DMA((2, 8)),
            sem, sem, sem, sem((2,)), sem((2,)), sem, sem,
        ]
        + [sems] * 11,
        compiler_params=pltpu.CompilerParams(
            collective_id=0, has_side_effects=True, vmem_limit_bytes=64 * 2**20 - 2**16
        ),
        name="exchange",
    )(
        owners,
        orbitals.reshape(2, ROWS, LEN),
        weights.reshape(LEN * PLANES, LEN),
        *[jnp.asarray(table) for table in tables()],
    )
    exchange, projector = pl.pallas_call(
        negate,
        out_shape=(
            jax.ShapeDtypeStruct((2, ROWS, LEN), jnp.float32),
            jax.ShapeDtypeStruct((COUNT, PLANES, LEN // BANDS, LEN), jnp.float32),
        ),
        in_specs=[vmem, vmem],
        out_specs=(vmem, vmem),
        name="negate",
    )(exchange, projector)
    return exchange.reshape(2, PLANES, LEN, LEN), projector


def solution(mesh):
    return jax.shard_map(
        shards,
        mesh=mesh,
        in_specs=(P("band", "fft", None, None), P(), P(None, "fft", None)),
        out_specs=(P("band", "fft", None, None), P(None, "fft", "band", None)),
        check_vma=False,
    )
```

```python
import functools

import jax
import jax.numpy as jnp
import ml_dtypes
import numpy as np
from jax import lax
from jax.experimental import pallas as pl
from jax.experimental.pallas import tpu as pltpu
from jax.sharding import PartitionSpec as P

MESH = pl.DeviceIdType.MESH
LEN = 128
COUNT = 4
GROUP = 32
BANDS = 8
ORDER = ((2, 2), (2, 1), (1, 2), (2, 3), (3, 2), (2, 0), (0, 2), (1, 1), (3, 3), (1, 3), (3, 1), (1, 0), (0, 1), (3, 0), (0, 3), (0, 0))
PLANES = 4
ROWS = PLANES * LEN


def halves(table):
    high = table.astype(ml_dtypes.bfloat16)
    low = (table - high.astype(np.float64)).astype(ml_dtypes.bfloat16)
    return high, low


def tables():
    n = np.arange(LEN)
    angle = 2.0 * np.pi * ((n[:, None] * n[None, :]) % LEN) / LEN
    cos, sin = np.cos(angle), np.sin(angle)
    forward = np.block([[cos, sin], [-sin, cos]])
    inverse = np.block([[cos, -sin], [sin, cos]])
    rows_y = np.arange(2 * LEN).reshape(2, GROUP, PLANES).transpose(1, 0, 2).reshape(-1)
    place, j = np.arange(GROUP)[:, None], np.arange(PLANES)[None, :]
    x, y_hi, y_lo, core = place // 8, place // 4 % 2, place // 2 % 2, place % 2
    plane = 64 * y_lo + 8 * (2 * j + 1 - core) + 4 * y_hi + x
    rows_x = np.stack([plane, plane + LEN], axis=-1).reshape(-1)

    def left(table):
        high, low = halves(table)
        return np.concatenate([high, low, high], axis=1)

    def right(table):
        high, low = halves(table)
        return np.concatenate([high, low, high], axis=0)

    return (
        right(forward.T),
        left(forward[rows_y]),
        left(forward[:, rows_x]),
        left(inverse[rows_x]),
        left(inverse[:, rows_y]),
        right(inverse.T),
    )


def parts(values):
    high = values.astype(jnp.bfloat16)
    low = (values - high.astype(jnp.float32)).astype(jnp.bfloat16)
    return high, low


def apply_left(table, values):
    high, low = parts(values)
    return jnp.dot(table, jnp.concatenate([high, high, low], axis=0), preferred_element_type=jnp.float32)


def apply_right(values, table):
    high, low = parts(values)
    return jnp.dot(jnp.concatenate([high, high, low], axis=1), table, preferred_element_type=jnp.float32)


def kernel(
    owners_in, orb_in, kern_in, fwd_z_in, fwd_y_in, fwd_x_in, inv_x_in, inv_y_in, inv_z_in,
    exch, proj,
    owners, orb, kern_own, fwd_z, fwd_y, fwd_x, inv_x, inv_y, inv_z, load_sem,
    res, inter, chosen, kern, fetched, c_send, c_recv, d_send, d_recv, total, partial, f_recv, shared_sum, br_sem,
    as_sem, ar_sem, bs_sem, ks_sem, kr_sem, es_sem, er_sem,
    gs_sem, gr_sem, gq_sem, cs_sem, cr_sem, ds_sem, dr_sem, fs_sem, fr_sem, ps_sem, pr_sem,
):
    band = lax.axis_index("band")
    pos = lax.axis_index("fft")
    x, y_hi = band // 2, band % 2
    y_lo, z, core = pos // 16, pos // 2 % 8, pos % 2
    half = LEN // 2
    block = PLANES * 8
    yrows = LEN // BANDS

    def device(to_band, to_y_lo, to_z, to_core):
        return (to_band, 16 * to_y_lo + 2 * to_z + to_core)

    def remote(src, dst, send, recv, target):
        return pltpu.make_async_remote_copy(
            src_ref=src, dst_ref=dst, send_sem=send, recv_sem=recv, device_id=target, device_id_type=MESH
        )

    def wait(ref, sem):
        pltpu.make_async_copy(ref, ref, sem).wait()

    def rows(index, size):
        return pl.ds(pl.multiple_of(index * size, size), size)

    def either(here, src, dst, recv, far_copy):
        @pl.when(here)
        def _():
            pltpu.make_async_copy(src, dst, recv).start()

        @pl.when(jnp.logical_not(here))
        def _():
            far_copy.start()

    loads = [
        pltpu.make_async_copy(src, dst, load_sem.at[k])
        for k, (src, dst) in enumerate(
            [(orb_in, orb), (owners_in, owners), (kern_in, kern_own), (fwd_z_in, fwd_z), (fwd_y_in, fwd_y),
             (fwd_x_in, fwd_x), (inv_x_in, inv_x), (inv_y_in, inv_y), (inv_z_in, inv_z)]
        )
    ]
    for load in loads[:3]:
        load.start()

    place = 4 * band + 2 * y_lo + core
    mine = 16 * y_lo + 2 * ((band - z + 8) % 8) + core

    barrier = pltpu.get_barrier_semaphore()

    def greet(target):
        pl.semaphore_signal(barrier, inc=1, device_id=target, device_id_type=MESH)

    def wrap(value, size):
        return jnp.where(value >= size, value - size, value)

    others = []
    step_by = jnp.where(core == 0, 1, 3)
    x_at = [x, wrap(x + step_by, 4), wrap(x + 2, 4), wrap(x + 4 - step_by, 4)]
    z_half = z // 2
    z_odd = z - 2 * z_half
    z_at = [wrap(z_half + 2, 4), wrap(z_half + 4 - step_by, 4), z_half, wrap(z_half + step_by, 4)]
    y_all = 2 * y_hi + y_lo
    y_at = []
    for value in (y_all, wrap(y_all + step_by, 4), wrap(y_all + 2, 4), wrap(y_all + 4 - step_by, 4)):
        upper = jnp.where(value >= 2, 1, 0)
        y_at.append((upper, value - 2 * upper))
    for dx, dy in ORDER:
        to_band = 2 * x_at[dx] + y_at[dy][0]
        to_y_lo = y_at[dy][1]
        to_zeta = wrap(to_band + 8 - z, 8)
        for flip in range(2):
            if (dx, dy, flip) != (0, 0, 0):
                to_core = core if flip == 0 else 1 - core
                others.append((
                    (to_band, 16 * to_y_lo + 2 * z + to_core),
                    4 * to_band + 2 * to_y_lo + to_core,
                    16 * to_y_lo + 2 * to_zeta + to_core,
                ))

    for target, _, _ in others:
        greet(target)

    @pl.loop(1, 16)
    def _(k):
        other = (2 * z + core + k) % 16
        greet((band, 16 * y_lo + other))

    greet(device((band + 4) % BANDS, y_lo, (band - z + 8) % 8, core))
    for load in loads[:3]:
        load.wait()
    for load in loads[3:]:
        load.start()
    total[...] = jnp.zeros_like(total)
    pl.semaphore_wait(barrier, GROUP - 1 + 15 + 1)

    for a in range(2):
        for n in (2, 1, 3, 0):
            for h in range(2):
                src = orb.at[a, rows(2 * x_at[n] + h, half)]
                dst = inter.at[2 * band + a]
                far_copy = remote(src, dst, bs_sem, br_sem.at[a, band], device(2 * x_at[n] + core, y_lo, z, h))
                if n > 0:
                    far_copy.start()
                else:
                    either((y_hi == core) & (core == h), src, dst, br_sem.at[a, band], far_copy)

    mirror = (band - z + 8) % 8
    across = (band + 4) % BANDS
    near, far = pl.ds(0, ROWS // 2), pl.ds(ROWS // 2, ROWS // 2)
    remote(
        kern_own.at[far], kern.at[far], ks_sem.at[1], kr_sem.at[1], device(across, y_lo, (across - z + 8) % 8, core)
    ).start()

    @pl.when(mirror == z)
    def _():
        pltpu.make_async_copy(kern_own.at[near], kern.at[near], kr_sem.at[0]).start()

    @pl.when(mirror != z)
    def _():
        remote(
            kern_own.at[near], kern.at[near], ks_sem.at[0], kr_sem.at[0], device(band, y_lo, mirror, core)
        ).start()

    def to_planes(odd, src, dst, send, recv):
        target_core = 1 - z_odd
        for n in range(4):
            to = 2 * z_at[n] + odd
            far_copy = remote(src(to), dst, send, recv, device(band, y_lo, to, target_core))
            if n != 2:
                far_copy.start()
            else:
                either((z_odd == odd) & (target_core == core), src(to), dst, recv, far_copy)

    slot = rows(2 * z_half + core, half)

    def select(i):
        chosen[i] = inter[owners[i]]

    relays = core == 1 - z_odd

    def spread(i):
        dst = fetched.at[i, slot]
        for step in (2, 6, 1, 7, 0):
            to = wrap(z + step, 8)
            recv = gq_sem.at[i] if step in (2, 6) else gr_sem.at[i]
            far_copy = remote(chosen.at[i], dst, gs_sem.at[i], recv, device(band, y_lo, to, 1 - z_odd))
            if step > 0:
                far_copy.start()
            else:
                either(relays, chosen.at[i], dst, recv, far_copy)

    def hand_on(i):
        @pl.when(relays)
        def _():
            wait(fetched.at[i, pl.ds(0, 4 * half)], gq_sem.at[i])
            for source, once, twice, kept in ((6, 1, 2, 0), (2, 7, 6, 1)):
                from_half = wrap(z + source, 8) // 2
                for h in (kept, 1 - kept):
                    held = fetched.at[i, rows(2 * from_half + h, half)]
                    for step in ((twice, once) if h == kept else (once,)):
                        remote(
                            held, held, gs_sem.at[i], gr_sem.at[i], device(band, y_lo, wrap(z + step, 8), core)
                        ).start()

    def fetched_here(i):
        @pl.when(relays)
        def _():
            wait(fetched.at[i, pl.ds(0, 4 * half)], gr_sem.at[i])

        @pl.when(jnp.logical_not(relays))
        def _():
            wait(fetched.at[i], gr_sem.at[i])

    def arrived(odd, a):
        for step in range(4):
            source = 2 * step + odd
            wait(inter.at[2 * source + a], br_sem.at[a, source])

    def resident(odd, a):
        to_planes(odd, lambda to: inter.at[2 * to + a], res.at[a, slot], as_sem, ar_sem)

    arrived(0, 0)
    resident(0, 0)
    arrived(0, 1)
    resident(0, 1)
    arrived(1, 0)
    arrived(1, 1)
    select(0)
    spread(0)
    resident(1, 0)
    resident(1, 1)
    for load in loads[3:]:
        load.wait()

    hand_on(0)
    wait(res, ar_sem)
    select(1)
    spread(1)

    @pl.loop(0, COUNT + 3)
    def _(step):
        @pl.when(step < COUNT)
        def _():
            i = step
            fetched_here(i)
            shared = fetched[i]
            density = jnp.concatenate([shared * res[0], shared * res[1]], axis=1)
            lines = apply_right(density, fwd_z[...])
            lines = lines.reshape(PLANES, LEN, 2 * LEN)
            stacked = jnp.concatenate(
                [jnp.concatenate([lines[p, :, :LEN], lines[p, :, LEN:]], axis=0) for p in range(PLANES)], axis=1
            )
            field = apply_left(fwd_y[...], stacked)
            out = jnp.stack([field[:, p * LEN : (p + 1) * LEN].reshape(GROUP, 8, LEN) for p in range(PLANES)], axis=1)
            c_send[i] = out.reshape(GROUP * block, LEN)

            for target, _, theirs in others:
                remote(
                    c_send.at[i, rows(theirs, block)], c_recv.at[i, rows(place, block)],
                    cs_sem.at[i], cr_sem.at[i], target,
                ).start()

            c_recv[i, rows(place, block)] = c_send[i, rows(mine, block)]

            @pl.when(step < COUNT - 1)
            def _():
                hand_on(step + 1)

            @pl.when(step < COUNT - 2)
            def _():
                select(step + 2)
                spread(step + 2)

        @pl.when((step >= 1) & (step < COUNT + 1))
        def _():
            i = step - 1

            @pl.when(i == 0)
            def _():
                wait(kern.at[near], kr_sem.at[0])
                wait(kern.at[far], kr_sem.at[1])

            wait(c_recv.at[i, pl.ds(0, block * (GROUP - 1))], cr_sem.at[i])
            columns = jnp.concatenate([c_recv[i, pl.ds(r, 2 * LEN, stride=4), :] for r in range(4)], axis=1)
            modes = apply_left(fwd_x[...], columns)
            scale = jnp.concatenate([kern[pl.ds(r, LEN, stride=4), :] for r in range(4)], axis=1) * (1.0 / LEN**3)
            modes = jnp.concatenate([modes[:LEN] * scale, modes[LEN:] * scale], axis=0)
            back = apply_left(inv_x[...], modes)
            for r in range(4):
                d_send[i, pl.ds(r, 2 * LEN, stride=4), :] = back[:, r * LEN : (r + 1) * LEN]

            for target, theirs, _ in others:
                remote(
                    d_send.at[i, rows(theirs, block)], d_recv.at[i, rows(mine, block)],
                    ds_sem.at[i], dr_sem.at[i], target,
                ).start()

            d_recv[i, rows(mine, block)] = d_send[i, rows(place, block)]

        @pl.when((step >= 2) & (step < COUNT + 2))
        def _():
            i = step - 2
            wait(d_recv.at[i, pl.ds(0, block * (GROUP - 1))], dr_sem.at[i])
            tiles = d_recv[i].reshape(GROUP, PLANES, 8, LEN)
            stacked = jnp.concatenate([tiles[:, p].reshape(2 * LEN, LEN) for p in range(PLANES)], axis=1)
            lines = apply_left(inv_y[...], stacked)
            flat = jnp.concatenate(
                [
                    jnp.concatenate(
                        [lines[:LEN, p * LEN : (p + 1) * LEN], lines[LEN:, p * LEN : (p + 1) * LEN]], axis=1
                    )
                    for p in range(PLANES)
                ],
                axis=0,
            )
            field = apply_right(flat, inv_z[...])
            one, two = field[:, :LEN], field[:, LEN:]
            shared = fetched[i]
            partial[i] = one * res[0] + two * res[1]

            for n in range(4):
                to_z = 2 * z_at[n] + 1 - core
                for to_core in range(2):
                    src = partial.at[i, rows(2 * z_at[n] + to_core, half)]
                    dst = f_recv.at[i, z]
                    far_copy = remote(src, dst, fs_sem.at[i], fr_sem.at[i], device(band, y_lo, to_z, to_core))
                    if n != 2:
                        far_copy.start()
                    else:
                        either((z_odd == 1 - core) & (core == to_core), src, dst, fr_sem.at[i], far_copy)

            total[0] += one * shared
            total[1] += two * shared

            @pl.when(i == COUNT - 1)
            def _():
                for j in z_at:
                    for a in range(2):
                        remote(
                            total.at[a, rows(j, LEN)], exch.at[a, rows(x, LEN)], es_sem, er_sem,
                            device(z, y_lo, 2 * j + 1 - core, y_hi),
                        ).start()

        @pl.when(step >= 3)
        def _():
            i = step - 3
            wait(f_recv.at[i], fr_sem.at[i])
            summed = f_recv[i, 0]
            for other in range(1, 8):
                summed += f_recv[i, other]
            shared_sum[i] = summed

            quarter = band % 4
            for k in range(4):
                part = wrap(quarter + k, 4)
                src = shared_sum.at[i, rows(part, yrows)]
                dst = proj.at[i, x]
                far_copy = remote(
                    src, dst, ps_sem.at[i], pr_sem.at[i], device(4 * core + part, y_lo, z, y_hi)
                )
                if k > 0:
                    far_copy.start()
                else:
                    either((band // 4 == core) & (y_hi == core), src, dst, pr_sem.at[i], far_copy)

    @pl.loop(0, COUNT)
    def _(i):
        wait(proj.at[i], pr_sem.at[i])

    wait(exch, er_sem)

    wait(total, es_sem)

    @pl.when(core == y_hi)
    def _():
        wait(inter.at[pl.ds(0, 14)], bs_sem)

    @pl.when(core != y_hi)
    def _():
        wait(inter, bs_sem)

    wait(kern.at[far], ks_sem.at[1])

    @pl.when(mirror != z)
    def _():
        wait(kern.at[near], ks_sem.at[0])

    @pl.when(core == 1 - z % 2)
    def _():
        wait(inter.at[pl.ds(0, 14)], as_sem)

    @pl.when(core == z % 2)
    def _():
        wait(inter, as_sem)

    @pl.loop(0, COUNT)
    def _(i):
        @pl.when(core == 1 - z % 2)
        def _():
            wait(fetched.at[i], gs_sem.at[i])
            wait(fetched.at[i, pl.ds(0, 2 * half)], gs_sem.at[i])

        @pl.when(core == z % 2)
        def _():
            wait(fetched.at[i, pl.ds(0, 5 * half)], gs_sem.at[i])

        wait(c_send.at[i, pl.ds(0, block * (GROUP - 1))], cs_sem.at[i])
        wait(d_send.at[i, pl.ds(0, block * (GROUP - 1))], ds_sem.at[i])

        @pl.when(core == 1 - z % 2)
        def _():
            wait(partial.at[i, pl.ds(0, ROWS - half)], fs_sem.at[i])

        @pl.when(core == z % 2)
        def _():
            wait(partial.at[i], fs_sem.at[i])

        @pl.when((core == band // 4) & (core == y_hi))
        def _():
            wait(proj.at[i, pl.ds(0, 3)], ps_sem.at[i])

        @pl.when((core != band // 4) | (core != y_hi))
        def _():
            wait(proj.at[i], ps_sem.at[i])


def negate(exchange, projector, exchange_out, projector_out):
    exchange_out[...] = -exchange[...]
    projector_out[...] = -projector[...]


def shards(orbitals, owners, weights):
    vmem = pl.BlockSpec(memory_space=pltpu.VMEM)
    wide = pltpu.VMEM((COUNT, GROUP * PLANES * 8, LEN), jnp.float32)
    local = pltpu.VMEM((COUNT, ROWS, LEN), jnp.float32)
    pair = pltpu.VMEM((2, ROWS, LEN), jnp.float32)
    single = pltpu.VMEM((ROWS, LEN), jnp.float32)
    spare = pltpu.VMEM((ROWS + 8, LEN), jnp.float32)
    wide_spare = pltpu.VMEM((COUNT, GROUP * PLANES * 8 + 8, LEN), jnp.float32)
    tall = pltpu.VMEM((6 * LEN, 2 * LEN), jnp.bfloat16)
    flat = pltpu.VMEM((2 * LEN, 6 * LEN), jnp.bfloat16)
    sem = pltpu.SemaphoreType.DMA
    sems = pltpu.SemaphoreType.DMA((COUNT,))
    exchange, projector = pl.pallas_call(
        kernel,
        out_shape=(
            jax.ShapeDtypeStruct((2, ROWS, LEN), jnp.float32),
            jax.ShapeDtypeStruct((COUNT, PLANES, LEN // BANDS, LEN), jnp.float32),
        ),
        in_specs=[pl.BlockSpec(memory_space=pltpu.HBM)] * 9,
        out_specs=(pl.BlockSpec(memory_space=pltpu.HBM),) * 2,
        scratch_shapes=[
            pltpu.SMEM((COUNT,), jnp.int32), pair, single,
            tall, flat, flat, flat, flat, tall,
            pltpu.SemaphoreType.DMA((9,)),
            pair,
            pltpu.VMEM((2 * BANDS, LEN // 2, LEN), jnp.float32),
            pltpu.VMEM((COUNT, LEN // 2, LEN), jnp.float32),
            spare, local, wide, wide_spare, wide_spare, wide, pair, local,
            pltpu.VMEM((COUNT, 8, LEN // 2, LEN), jnp.float32),
            pltpu.VMEM((COUNT, LEN // 2, LEN), jnp.float32),
            pltpu.SemaphoreType.DMA((2, 8)),
            sem, sem, sem, sem((2,)), sem((2,)), sem, sem,
        ]
        + [sems] * 11,
        compiler_params=pltpu.CompilerParams(
            collective_id=0, has_side_effects=True, vmem_limit_bytes=64 * 2**20 - 2**16
        ),
        name="exchange",
    )(
        owners,
        orbitals.reshape(2, ROWS, LEN),
        weights.reshape(LEN * PLANES, LEN),
        *[jnp.asarray(table) for table in tables()],
    )
    exchange, projector = pl.pallas_call(
        negate,
        out_shape=(
            jax.ShapeDtypeStruct((2, ROWS, LEN), jnp.float32),
            jax.ShapeDtypeStruct((COUNT, PLANES, LEN // BANDS, LEN), jnp.float32),
        ),
        in_specs=[vmem, vmem],
        out_specs=(vmem, vmem),
        name="negate",
    )(exchange, projector)
    return exchange.reshape(2, PLANES, LEN, LEN), projector


def solution(mesh):
    return jax.shard_map(
        shards,
        mesh=mesh,
        in_specs=(P("band", "fft", None, None), P(), P(None, "fft", None)),
        out_specs=(P("band", "fft", None, None), P(None, "fft", "band", None)),
        check_vma=False,
    )
```
